32 devices in a mesh: section: 2 (over core), mp: 4 (over z), dp: 4 (over y, x).
Axes of the slice: x: 2, y: 2, z: 4, core: 2. Of those that a mesh axis runs over, the one named last changes fastest.
Arguments:
- tokens: bfloat16 [48, 512, 512], P('dp', 'mp'), may hold values from -6 to 6
- valid: int32 [48], P('dp'), may hold values 0 or 1
- conv_weight: bfloat16 [2, 9, 512, 512], P('section', None, None, 'mp'), may hold values from -0.09375 to 0.09375
- gain_one: float32 [2, 512], P('section'), may hold values from 0.25 to 1.75
- gain_two: float32 [2, 512], P('section'), may hold values from 0.25 to 1.75
- up_weight: bfloat16 [2, 512, 2048], P('section', None, 'mp'), may hold values from -0.25 to 0.25
- down_weight: bfloat16 [2, 2048, 512], P('section', 'mp'), may hold values from -0.125 to 0.125
- cotangent: bfloat16 [48, 512, 512], P('dp', 'mp'), may hold values from -6 to 6
Outputs:
- block_outputs: bfloat16 [2, 48, 512, 512], P('section', 'dp', 'mp')
- input_grads: bfloat16 [2, 48, 512, 512], P('section', 'dp', 'mp')
- conv_grad: float32 [2, 9, 512, 512], P('section', None, None, 'mp')
- gain_one_grad: float32 [2, 512], P('section', 'mp')
- gain_two_grad: float32 [2, 512], P('section', 'mp')
- up_grad: float32 [2, 512, 2048], P('section', None, 'mp')
- down_grad: float32 [2, 2048, 512], P('section', 'mp')
The draws below stay inside these ranges and needn't reach their ends.
All inputs are finite; a program needn't handle non-finite values. No bound on the sum of `valid` on one device may be relied on, other than what follows from the above.
Results may differ from the reference program's by a relative error of at most 0.02.
Values may be sent and summed in bfloat16 or wider, within the bound.
A program may use at most 256 MiB of HBM per device.

```python
import math
import jax
import jax.numpy as jnp
from jax import lax

D = 512
FF = 2048
KERNEL = 9
DILATION = 32
SEQ = 512
WINDOWS = 48


def with_ends(result, own_key, smallest, top_value):
    index_at = [jax.random.randint(jax.random.fold_in(own_key, axis), (), 0, length) for axis, length in enumerate(result.shape)]
    longest = result.shape.index(max(result.shape))
    beside = index_at[:longest] + [(index_at[longest] + 1) % result.shape[longest]] + index_at[longest + 1:]
    return result.at[tuple(index_at)].set(smallest).at[tuple(beside)].set(top_value)


def level_of(stream_key, shape, cuts, low, largest):
    level, own = 1.0, jax.random.fold_in(stream_key, 6)
    for dim, shards_of in cuts:
        draws = jnp.exp(jax.random.uniform(jax.random.fold_in(own, dim), (shards_of,), jnp.float32, low / len(cuts), largest / len(cuts)))
        level = level * jnp.repeat(draws, shape[dim] // shards_of).reshape([-1 if axis == dim else 1 for axis in range(len(shape))])
    return level


def bell_draw(rng, extent, width, most, split=(), dtype=jnp.bfloat16):
    level = level_of(rng, extent, split, -0.22, 0.18) if split else 1.0
    entries = jax.random.normal(rng, extent, jnp.float32) * width * level
    return jnp.minimum(jnp.maximum(entries, -most), most).astype(dtype)


def setup_inputs(seed: int = 0) -> dict:
    arg_keys = jax.random.split(jax.random.key(seed), 9)
    tokens = bell_draw(arg_keys[0], (WINDOWS, SEQ, D), 1.0, 6.0, ((0, 4), (1, 4)))
    valid = with_ends((jax.random.randint(arg_keys[1], (WINDOWS,), 0, 4) < 3).astype(jnp.int32), jax.random.fold_in(arg_keys[1], 1), 0, 1)
    conv_weight = bell_draw(arg_keys[2], (2, KERNEL, D, D), (KERNEL * D) ** -0.5, 0.09375, ((0, 2), (3, 4)))
    gain_one = jnp.clip(1.0 + 0.15 * jax.random.normal(arg_keys[3], (2, D), jnp.float32), 0.25, 1.75)
    gain_two = jnp.clip(1.0 + 0.15 * jax.random.normal(arg_keys[4], (2, D), jnp.float32), 0.25, 1.75)
    up_weight = bell_draw(arg_keys[5], (2, D, FF), D ** -0.5, 0.25, ((0, 2), (2, 4)))
    down_weight = bell_draw(arg_keys[6], (2, FF, D), FF ** -0.5, 0.125, ((0, 2), (1, 4)))
    cotangent = bell_draw(arg_keys[7], (WINDOWS, SEQ, D), 1.0, 6.0, ((0, 4), (1, 4)))
    return dict(tokens=tokens, valid=valid, conv_weight=conv_weight, gain_one=gain_one, gain_two=gain_two, up_weight=up_weight, down_weight=down_weight, cotangent=cotangent)


@jax.custom_vjp
def low(v):
    return lax.optimization_barrier(v.astype(jnp.bfloat16)).astype(jnp.float32)

@jax.custom_vjp
def low_back(v):
    return v

def low_keep(v):
    return (low(v), None)

def low_pass(kept, grad):
    return (grad,)

def back_keep(v):
    return (v, None)

def back_low(kept, grad):
    return (low(grad),)
low.defvjp(low_keep, low_pass)
low_back.defvjp(back_keep, back_low)

def normed(values, gain):
    center = values - lax.optimization_barrier(jnp.mean(values, axis=-1, keepdims=True))
    spread = lax.optimization_barrier(jnp.mean(center * center, axis=-1, keepdims=True))
    return center * lax.rsqrt(spread + 1e-05) * gain

def dilated(inputs, kernel, dilation):
    margin = KERNEL // 2 * dilation
    padded = jnp.pad(inputs, ((0, 0), (margin, margin), (0, 0)))
    total = jnp.zeros(inputs.shape[:2] + (kernel.shape[2],), jnp.float32)
    for tap in range(KERNEL):
        window = padded[:, tap * dilation:tap * dilation + SEQ]
        total = total + jnp.einsum('wsd,de->wse', window, kernel[tap], precision=lax.Precision.HIGHEST)
    return total

def block(inputs, weights, kernel, gain_a, gain_b, up_w, down_w, dilation):
    normed_in = low(normed(inputs, gain_a))
    conv_out = low_back(dilated(normed_in, kernel, dilation))
    activated = low_back(low(jax.nn.gelu(conv_out)))
    middle = inputs + weights * activated
    ffn_in = low(normed(middle, gain_b))
    pre = low_back(jnp.einsum('wsd,dh->wsh', ffn_in, up_w, precision=lax.Precision.HIGHEST))
    hidden = low(jax.nn.gelu(pre))
    branch = low_back(jnp.einsum('wsh,hd->wsd', hidden, down_w, precision=lax.Precision.HIGHEST))
    return middle + weights * branch

def reference(tokens, valid, conv_weight, gain_one, gain_two, up_weight, down_weight, cotangent):
    group = math.gcd(WINDOWS, max(1, 4096 // SEQ))
    steps_count = WINDOWS // group
    weights = valid.astype(jnp.float32).reshape(steps_count, group, 1, 1)

    def forward(inputs, kernel, gain_a, gain_b, up_w, down_w, probe):

        def step(carry, items):
            x_group, mask_group, probe_group = items
            first = block(x_group, mask_group, kernel[0], gain_a[0], gain_b[0], up_w[0], down_w[0], 1)
            second_in = low_back(low(first)) + probe_group
            second = block(second_in, mask_group, kernel[1], gain_a[1], gain_b[1], up_w[1], down_w[1], DILATION)
            return (carry, (first, second))
        shaped = (steps_count, group, SEQ, D)
        _, (first, second) = lax.scan(jax.checkpoint(step), jnp.float32(0.0), (inputs.reshape(shaped), weights, probe.reshape(shaped)))
        return (second.reshape(WINDOWS, SEQ, D), first.reshape(WINDOWS, SEQ, D))
    inputs = tokens.astype(jnp.float32)
    probe = jnp.zeros_like(inputs)
    second, pull, first = jax.vjp(forward, inputs, conv_weight.astype(jnp.float32), gain_one, gain_two, up_weight.astype(jnp.float32), down_weight.astype(jnp.float32), probe, has_aux=True)
    grad_x, grad_conv, grad_one, grad_two, grad_up, grad_down, grad_probe = pull(cotangent.astype(jnp.float32))
    outputs = jnp.stack([first, second]).astype(jnp.bfloat16)
    in_grads = jnp.stack([grad_x, grad_probe]).astype(jnp.bfloat16)
    return (outputs, in_grads, grad_conv, grad_one, grad_two, grad_up, grad_down)
```

```python
import jax
import jax.numpy as jnp
from jax import lax
from jax.experimental import pallas as pl
from jax.experimental.pallas import tpu as pltpu
from jax.sharding import PartitionSpec as P

KERNEL = 9
DILATION = 32
HALF = KERNEL // 2
PHASES = 8
TILE = 16
COLS = 256
C0 = 0.7978845608028654
C1 = 0.044715
BF = jnp.bfloat16
F32 = jnp.float32
MESH = pl.DeviceIdType.MESH
LATENCY = 2.0
NEVER = 1e9
AHEAD = 1.0
Z_FIRST = (7,)


def gelu_and_slope(v):
    v2 = v * v
    t = jnp.tanh(v * (C0 + (C0 * C1) * v2))
    h = 0.5 + 0.5 * t
    slope = h + v * (1.0 - t * t) * (0.5 * C0 + (1.5 * C0 * C1) * v2)
    return v * h, slope


def norm_parts(values):
    center = values - jnp.mean(values, axis=-1, keepdims=True)
    r = lax.rsqrt(jnp.mean(center * center, axis=-1, keepdims=True) + 1e-05)
    return center * r, r


def norm_back(g, hat, r):
    return r * (
        g
        - jnp.mean(g, axis=-1, keepdims=True)
        - hat * jnp.mean(g * hat, axis=-1, keepdims=True)
    )


def dot(a, b):
    return jnp.dot(a, b, preferred_element_type=F32)


def dot_nt(a, b):
    return lax.dot_general(a, b, (((1,), (1,)), ((), ())), preferred_element_type=F32)


def make_kernel(mp, dp, nw, seq, width):
    levels = dp.bit_length() - 1
    assert dp == 1 << levels and 2 <= levels <= 4
    rows_all = nw * seq
    q_count = seq // PHASES
    group_rows = width // mp
    half_rows = group_rows // 2
    nblk = KERNEL + 2 * mp
    margin = HALF * DILATION
    conv_groups = [(0, 3), (3, 3), (6, 3)]
    wgroups = [(b, g) for b in range(2) for g in conv_groups + [(KERNEL, mp), (KERNEL + mp, mp)]]
    back_groups = [(0, 3), (3, 3), (6, 2), (8, 1)]
    ggroups = [(b, g) for b in (1, 0) for g in [(KERNEL + mp, mp), (KERNEL, mp)] + back_groups]
    per_grad = len(back_groups) + 2
    z_order = list(Z_FIRST)
    assert len(z_order) <= 2
    z_first = {g: i % 2 for i, g in enumerate(z_order)}
    batches = 3 if nw % 3 == 0 else 1
    wb = nw // batches
    nwg, ngg = len(wgroups), len(ggroups)
    per_block = len(conv_groups) + 2
    piece_cols = width if levels == 2 else width >> (levels - 2)

    def body(tok, cot, valid, one_in, two_in, conv_in, up_in, down_in,
             blk, ing, fin, gout_sum, sp_hid, sp_slo,
             big, recv_c, recv_z, recv_zf, piece, xext, xpad, gpad, hid, slo, x0, x1, x2, midb, ffn,
             slope1, gout, gb, tra, trb, acc, mid, ig1, gains, slab, edge, hsend, hrecv,
             gbuf, grecv, *rest):
        recv_x = rest[:levels]
        (agz_s, agz_r, agf_s, agx_s, agx_r, agk_s, agk_r, own_l, own_s, own_r, rc_s, rc_r, rx_s, rx_r,
         rz_s, rz_r, zf_s, zf_r, rf_s, rf_r, gn_s, gn_r, halo_s, halo_r, out_s, out_r, loc, credit) = rest[levels:]
        s = lax.axis_index("section")
        m = lax.axis_index("mp")
        d = lax.axis_index("dp")

        def dev(ss, mm, dd):
            return {"section": ss, "mp": mm, "dp": dd}

        sibling = dev(1 - s, m, d)

        flipped = 0
        for j in range(levels):
            flipped = flipped + ((d // (1 << j)) % 2) * (1 << (levels - 1 - j))
        place = (1 - s) * d + s * flipped

        def bit(j):
            return (place // (1 << j)) % 2

        def partner(j):
            other = (1 - s) * (1 << j) + s * (1 << (levels - 1 - j))
            has = (d // other) % 2
            return dev(s, m, d + other - 2 * other * has)

        def peer(k):
            return lax.rem(m + k, mp)

        def rcopy(src, dst, ssem, rsem, device):
            return pltpu.make_async_remote_copy(
                src_ref=src, dst_ref=dst, send_sem=ssem, recv_sem=rsem,
                device_id=device, device_id_type=MESH)

        sends = []

        def begin(copy, cond=None, kind=None):
            if cond is None:
                copy.start()
            else:
                pl.when(cond)(copy.start)
            sends.append((copy, cond, kind))

        def flush(kind=None):
            for copy, cond, its in [x for x in sends if kind is None or x[2] == kind]:
                if cond is None:
                    copy.wait_send()
                else:
                    pl.when(cond)(copy.wait_send)
            sends[:] = [x for x in sends if kind is not None and x[2] != kind]

        barrier = pltpu.get_barrier_semaphore()
        count = 0
        for o in range(dp):
            for ss in range(2):
                if o == 0 and ss == 0:
                    continue
                other = d + o - dp * ((d + o) // dp)
                pl.semaphore_signal(
                    barrier, inc=1, device_id=dev(s + ss - 2 * s * ss, m, other), device_id_type=MESH)
                count += 1
        for k in range(1, mp):
            for ss in range(2):
                pl.semaphore_signal(
                    barrier, inc=1, device_id=dev(s + ss - 2 * s * ss, peer(k), d), device_id_type=MESH)
                count += 1
        loads = [
            pltpu.make_async_copy(tok.at[pl.ds(s * nw, nw)], x1, loc.at[0]),
            pltpu.make_async_copy(one_in, gains.at[s, 0], loc.at[1]),
            pltpu.make_async_copy(two_in, gains.at[s, 1], loc.at[2]),
            pltpu.make_async_copy(cot.at[pl.ds(s * nw, nw)], gout, loc.at[3]),
        ]
        for copy in loads:
            copy.start()
        pl.semaphore_wait(barrier, count)

        def shard_view(b, group, mm):
            j0, nj = group
            if j0 < KERNEL:
                return big.at[b, pl.ds(j0, nj), :, :, pl.ds(pl.multiple_of(mm * group_rows, group_rows), group_rows)]
            return big.at[b, j0 + mm]

        def own_source(group):
            j0, nj = group
            if j0 < KERNEL:
                return conv_in.at[pl.ds(j0, nj)]
            return up_in if j0 == KERNEL else down_in

        def sub(ref, half, at, level):
            lead = ref.shape[:-3]
            idx = (slice(None),) * len(lead)
            step = half_rows // min(dp, 4)
            if levels == 2:
                first = ((at // (1 << level)) * (1 << level)) * step
                return ref.at[idx + (slice(None), pl.ds(pl.multiple_of(half * half_rows + first, TILE), step << level))]
            low, high = at % 4, at // 4
            if level <= 2:
                first = ((low // (1 << level)) * (1 << level)) * step
                return ref.at[idx + (pl.ds(high, 1), pl.ds(pl.multiple_of(half * half_rows + first, TILE), step << level))]
            up = level - 2
            first = (high // (1 << up)) * (1 << up)
            return ref.at[idx + (pl.ds(first, 1 << up), pl.ds(pl.multiple_of(half * half_rows, TILE), half_rows))]

        def place_of(half):
            return d if half == 0 else flipped

        own = []
        for i, group in enumerate(conv_groups + [(KERNEL, mp), (KERNEL + mp, mp)]):
            src, dst = own_source(group), shard_view(s, group, m)
            local = pltpu.make_async_copy(src, dst, own_l.at[i])
            local.start()
            own.append(local)
        begin(rcopy(one_in, gains.at[s, 0], gn_s.at[0], gn_r.at[0], sibling))
        begin(rcopy(two_in, gains.at[s, 1], gn_s.at[levels + mp], gn_r.at[levels + mp], sibling))

        def z_copies(n):
            b, group = wgroups[n]
            i = n % per_block
            out = [(rcopy(own_source(group), shard_view(b, group, m), own_s.at[i], own_r.at[i], sibling), None)]
            for k in (2, 1, 3):
                for half in range(2):
                    copy = rcopy(
                        sub(own_source(group), half, place_of(half), 0),
                        sub(shard_view(b, group, m), half, place_of(half), 0),
                        agz_s.at[i, k - 1, half], agz_r.at[n, k - 1], dev(half, peer(k), d))
                    out.append((copy, None if k == 2 else (m != 3 if k == 1 else m != 0)))
            return out

        def z_send(n):
            @pl.when(s == wgroups[n][0])
            def _():
                for copy, cond in z_copies(n):
                    if cond is None:
                        copy.start()
                    else:
                        pl.when(cond)(copy.start)

        def z_flush(n):
            @pl.when(s == wgroups[n][0])
            def _():
                for copy, cond in z_copies(n):
                    if cond is None:
                        copy.wait_send()
                    else:
                        pl.when(cond)(copy.wait_send)

        def received(dst, rsem):
            rcopy(dst, dst, rsem, rsem, sibling).wait_recv()

        def z_forward(n):
            b, group = wgroups[n]
            held = sub(shard_view(b, group, peer(mp - 2)), s, place, 0)
            received(held, agz_r.at[n, 1])
            for at, to, k in ((2, 3, 3), (1, 0, 1)):
                begin(rcopy(held, held, agf_s.at[n], agz_r.at[n, k - 1], dev(s, to, d)), m == at, ("gather", b))

        def run_view(b, group, first, count):
            j0, nj = group
            if j0 < KERNEL:
                return big.at[b, pl.ds(j0, nj), :, :, pl.ds(first * group_rows, count * group_rows)]
            return big.at[b, pl.ds(j0 + first, count)]

        def foreign(n, half, at, level):
            b, group = wgroups[n]
            return sub(run_view(b, group, 0, mp - 1), half, at, level)

        def x_step(n, level):
            b, group = wgroups[n]
            if level == 0:
                for k in (1, 3):
                    received(sub(shard_view(b, group, peer(mp - k)), s, place, 0), agz_r.at[n, k - 1])
            else:
                received(foreign(n, s, place, level - 1), agx_r.at[n, level - 1])
            if level < levels:
                sems, to = (agx_s.at[n, level], agx_r.at[n, level]), partner(level)
            else:
                sems, to = (agk_s.at[n], agk_r.at[n]), sibling
            for mine in range(mp):
                @pl.when(m == mine)
                def _():
                    for first, count in ((0, mine), (mine + 1, mp - 1 - mine)):
                        if count:
                            part = sub(run_view(b, group, first, count), s, place, level)
                            rcopy(part, part, *sems, to).start()
            held = foreign(n, s, place, level)
            sends.append((rcopy(held, held, *sems, to), None, ("gather", b)))

        def gathered(n):
            b, group = wgroups[n]
            i = n % per_block

            @pl.when(s == b)
            def _():
                pltpu.make_async_copy(own_source(group), shard_view(b, group, m), own_l.at[i]).wait()

            @pl.when(s != b)
            def _():
                received(shard_view(b, group, m), own_r.at[i])

            received(foreign(n, 1 - s, 0, levels), agk_r.at[n])

        clock = {"now": 4.0}
        gate = {"open": False}
        busy = {}
        chains = {}

        def post(link, size, rate):
            start = max(clock["now"], busy.get(link, 0.0))
            busy[link] = start + size / rate
            return busy[link] + LATENCY

        def resume(key):
            try:
                chains[key][0] = next(chains[key][1])
            except StopIteration:
                del chains[key]

        def launch(key, chain):
            chains[key] = [0.0, chain]
            resume(key)

        def service():
            while True:
                ready = [(c[0], key) for key, c in chains.items()
                         if c[0] <= clock["now"] + (AHEAD if key[0] == 0 and key[1] < per_block else 0.0)]
                if not ready:
                    return
                when, key = min(ready)
                clock["now"] = max(clock["now"], when)
                resume(key)

        def complete(keys):
            while any(key in chains for key in keys):
                when, key = min((c[0], key) for key, c in chains.items())
                clock["now"] = max(clock["now"], when)
                resume(key)

        def work(cost, call, *args):
            call(*args)
            clock["now"] += cost
            service()

        def gather_chain(n):
            b, group = wgroups[n]
            unit = (group[1] * width * group_rows if group[0] < KERNEL else width * width) * 2 / (2 * dp) / 1e3
            yield post("z", 6 * unit, 100)
            if n == per_block - 2:
                for later in range(per_block, nwg):
                    begin_gather(later)
            if b == 1 and not gate["open"]:
                yield NEVER
            z_forward(n)
            yield clock["now"] + LATENCY
            x_step(n, 0)
            when = post("xy", 3 * unit, 100)
            for level in range(1, levels):
                yield when
                x_step(n, level)
                when = post("xy", 3 * unit * (1 << level), 100)
            if n == per_block - 1:
                gate["open"] = True
                for chain in chains.values():
                    if chain[0] == NEVER:
                        chain[0] = clock["now"]
            yield when
            x_step(n, levels)
            yield post("core", 3 * unit * dp, 500)
            gathered(n)

        def begin_gather(n):
            z_send(n)
            launch((0, n), gather_chain(n))

        begin_gather(0)

        def halo_pairs(index, batch):
            if index % 2 == 0:
                up = (hsend.at[0], hrecv.at[0])
                down = (hsend.at[1], hrecv.at[1])
            else:
                ref = xpad if index == 1 else gpad
                part = pl.ds(batch * wb, wb)
                mine = ref.at[part, pl.ds(margin, seq)]
                up = (mine, ref.at[part, pl.ds(0, margin)])
                down = (mine, ref.at[part, pl.ds(margin + seq, margin)])
            return up, down

        def halo_send(index, batch=0):
            up, down = halo_pairs(index, batch)
            begin(rcopy(up[0], up[1], halo_s.at[index, batch, 0], halo_r.at[index, batch, 0],
                        dev(s, lax.rem(m + 1, mp), d)), m < mp - 1, "halo")
            begin(rcopy(down[0], down[1], halo_s.at[index, batch, 1], halo_r.at[index, batch, 1],
                        dev(s, lax.rem(m + mp - 1, mp), d)), m > 0, "halo")
            return post("z", (wb * seq * width * 2 / 1e3) if index % 2 else 98.0, 50)

        def halo_wait(index, batch=0, when=0.0):
            while chains and min(c[0] for c in chains.values()) <= when:
                first, key = min((c[0], key) for key, c in chains.items())
                clock["now"] = max(clock["now"], first)
                resume(key)
            clock["now"] = max(clock["now"], when)
            up, down = halo_pairs(index, batch)
            pl.when(m > 0)(lambda: received(up[1], halo_r.at[index, batch, 0]))
            pl.when(m < mp - 1)(lambda: received(down[1], halo_r.at[index, batch, 1]))

        def zero_edges(ref):
            @pl.when(m == 0)
            def _():
                ref[:, :margin] = jnp.zeros((nw, margin, width), BF)

            @pl.when(m == mp - 1)
            def _():
                ref[:, margin + seq:] = jnp.zeros((nw, margin, width), BF)

        def tile(j):
            return pl.ds(j * q_count, q_count)

        def stage_edges(ext):
            @pl.loop(0, nw)
            def _(w):
                for j in range(HALF):
                    last = ext[w, tile(PHASES + j), :].astype(F32)
                    hsend[0, w, pl.ds(j, 1), :] = last[q_count - 1:, :]
                    first = ext[w, tile(HALF + j), :].astype(F32)
                    hsend[1, w, pl.ds(j, 1), :] = first[:1, :]

        def fill_edges(ext):
            @pl.when(m == 0)
            def _():
                hrecv[0] = jnp.zeros((nw, 8, width), F32)

            @pl.when(m == mp - 1)
            def _():
                hrecv[1] = jnp.zeros((nw, 8, width), F32)

            @pl.loop(0, nw)
            def _(w):
                for j in range(HALF):
                    edge[j, pl.ds(8, q_count), :] = ext[w, tile(PHASES + j), :].astype(F32)
                    edge[j, pl.ds(7, 1), :] = hrecv[0, w, pl.ds(j, 1), :]
                    ext[w, tile(j), :] = edge[j, pl.ds(7, q_count), :].astype(BF)
                    edge[HALF + j, pl.ds(8, q_count), :] = ext[w, tile(HALF + j), :].astype(F32)
                    edge[HALF + j, pl.ds(8 + q_count, 1), :] = hrecv[1, w, pl.ds(j, 1), :]
                    ext[w, tile(HALF + PHASES + j), :] = edge[HALF + j, pl.ds(9, q_count), :].astype(BF)

        def to_phases(value, store):
            for c in range(width // 128):
                slab[c] = value[:, c * 128:(c + 1) * 128]
            for r in range(PHASES):
                store(r, jnp.concatenate(
                    [slab[c, pl.ds(r, q_count, stride=PHASES), :] for c in range(width // 128)], axis=1))

        def from_phases(value):
            for r in range(PHASES):
                for c in range(width // 128):
                    slab[c, pl.ds(r, q_count, stride=PHASES), :] = (
                        value[r * q_count:(r + 1) * q_count, c * 128:(c + 1) * 128])
            return jnp.concatenate([slab[c] for c in range(width // 128)], axis=1)

        def window_mask(w):
            return valid[s * nw + w].astype(F32)

        def shifted(ref, b, k, batch):
            first = k * (q_count if b == 0 else DILATION)
            if not isinstance(k, int):
                first = pl.multiple_of(first, TILE)
            if batch is None:
                return ref[:, pl.ds(first, seq), :].reshape(rows_all, width)
            return ref[pl.ds(batch * wb, wb), pl.ds(first, seq), :].reshape(wb * seq, width)

        def tap(b, k, batch=None):
            return shifted(xext if b == 0 else xpad, b, k, batch)

        def gtap(b, k, batch=None):
            return shifted(gpad, b, k, batch)

        def part_rows(batch):
            return slice(None) if batch is None else pl.ds(batch * wb * seq, wb * seq)

        def part_windows(batch):
            return (0, nw) if batch is None else (batch * wb, (batch + 1) * wb)

        def cols_of(n):
            return pl.ds(pl.multiple_of(n * COLS, COLS), COLS)

        def first_norm(b, batch=None):
            @pl.loop(*part_windows(batch))
            def _(w):
                if b == 0:
                    def keep(r, tile):
                        x0[w, pl.ds(r * q_count, q_count), :] = tile.astype(BF)
                    to_phases(x1[w].astype(F32), keep)
                    x = x0[w]
                else:
                    x = x1[w]
                hat, _r = norm_parts(x.astype(F32))
                n = (hat * gains[b, 0]).astype(BF)
                if b == 0:
                    xext[w, pl.ds(HALF * q_count, seq), :] = n
                else:
                    xpad[w, pl.ds(margin, seq), :] = n

        def conv_part(b, taps, batch, n):
            rows, cols = part_rows(batch), pl.ds(n * COLS, COLS)
            total = None
            for k in taps:
                wk = big[b, k, :, :, cols].reshape(width, COLS)
                term = dot(tap(b, k, batch), wk)
                total = term if total is None else total + term
            if taps[0]:
                total = total + acc[rows, cols]
            acc[rows, cols] = total

        def rows_of(w):
            return pl.ds(pl.multiple_of(w * seq, seq), seq)

        def middle(b, batch=None):
            x = x0 if b == 0 else x1

            @pl.loop(*part_windows(batch))
            def _(w):
                act, slope = gelu_and_slope(acc[rows_of(w), :])
                slope1[b, w] = slope.astype(BF)
                value = x[w].astype(F32) + window_mask(w) * act.astype(BF).astype(F32)
                if b == 0:
                    mid[w] = value
                midb[b, w] = value.astype(BF)
                hat, _r = norm_parts(value)
                ffn[b, rows_of(w), :] = (hat * gains[b, 1]).astype(BF)

        def up(b, batch, quarter, quarters):
            count = mp * width // COLS // quarters
            rows = part_rows(batch)

            @pl.loop(quarter * count, (quarter + 1) * count)
            def _(n):
                per = width // COLS
                wk = big[b, KERNEL + n // per, :, :, cols_of(lax.rem(n, per))].reshape(width, COLS)
                h, slope = gelu_and_slope(dot(ffn[b, rows, :], wk))
                hid[rows, cols_of(n)] = h.astype(BF)
                slo[rows, cols_of(n)] = slope.astype(BF)

        def down(b, batch):
            rows = part_rows(batch)

            @pl.loop(0, width // COLS)
            def _(n):
                total = None
                for mm in range(mp):
                    wk = big[b, KERNEL + mp + mm, :, :, cols_of(n)].reshape(width, COLS)
                    term = dot(hid[rows, mm * width:(mm + 1) * width], wk)
                    total = term if total is None else total + term
                acc[rows, cols_of(n)] = total

        def down_out(b, batch):
            @pl.loop(*part_windows(batch))
            def _(w):
                branch = window_mask(w) * acc[rows_of(w), :]
                if b == 0:
                    x1[w] = from_phases(mid[w] + branch).astype(BF)
                else:
                    x2[w] = (midb[b, w].astype(F32) + branch).astype(BF)

        def send_home(ref, target, b, index):
            dst = target.at[pl.ds(s * nw, nw)]

            @pl.when(s == b)
            def _():
                pltpu.make_async_copy(ref, dst, out_s.at[index]).start()

            @pl.when(s != b)
            def _():
                rcopy(ref, dst, out_s.at[index], out_r.at[index], sibling).start()

        def sent_home(ref, target, b, index):
            dst = target.at[pl.ds(s * nw, nw)]

            @pl.when(s == b)
            def _():
                pltpu.make_async_copy(ref, dst, out_s.at[index]).wait()
                received(target.at[pl.ds((1 - s) * nw, nw)], out_r.at[index])

            @pl.when(s != b)
            def _():
                rcopy(ref, dst, out_s.at[index], out_r.at[index], sibling).wait_send()

        def slot(b):
            return 2 if b == 1 else 1

        def branch_grad(b):
            @pl.loop(0, nw)
            def _(w):
                value = window_mask(w) * gout[w].astype(F32)
                low = value.astype(BF)
                gb[rows_of(w), :] = low
                tra[:, rows_of(w)] = low.T

        def transposed_ffn(b):
            @pl.loop(0, nw)
            def _(w):
                trb[:, rows_of(w)] = ffn[b, rows_of(w), :].T

        def wide(n):
            return pl.ds(pl.multiple_of(n * width, width), width)

        def down_grad(b):
            @pl.loop(0, mp)
            def _(n):
                part = dot(tra[...], hid[:, wide(n)])
                big[slot(b), KERNEL + mp + n] = part.astype(BF).reshape(mp, group_rows, width)

        def pre_grad(b):
            @pl.loop(0, mp * width // COLS)
            def _(n):
                per = width // COLS
                span = COLS // group_rows
                wk = big[b, KERNEL + mp + n // per, pl.ds(lax.rem(n, per) * span, span)].reshape(COLS, width)
                g = dot_nt(gb[...], wk) * slo[:, cols_of(n)].astype(F32)
                slo[:, cols_of(n)] = g.astype(BF)

        def up_grad(b):
            @pl.loop(0, mp)
            def _(n):
                part = dot(trb[...], slo[:, wide(n)])
                big[slot(b), KERNEL + n] = part.astype(BF).reshape(mp, group_rows, width)

        def ffn_grad(b):
            span = COLS // group_rows

            @pl.loop(0, width // COLS)
            def _(n):
                total = None
                for mm in range(mp):
                    wk = big[b, KERNEL + mm, pl.ds(n * span, span)].reshape(COLS, width)
                    term = dot_nt(slo[:, mm * width:(mm + 1) * width], wk)
                    total = term if total is None else total + term
                acc[:, cols_of(n)] = total

        def ffn_back(b, batch):
            @pl.loop(*part_windows(batch))
            def _(w):
                gf = acc[rows_of(w), :]
                hat, r = norm_parts(midb[b, w].astype(F32))
                gbuf[0, b, 1:2, :] += jnp.sum(gf * hat, axis=0, keepdims=True)
                gm = gout[w].astype(F32) + norm_back(gf * gains[b, 1], hat, r)
                mid[w] = gm
                ga = (window_mask(w) * gm).astype(BF).astype(F32)
                gc = ga * slope1[b, w].astype(F32)
                low = gc.astype(BF)
                if b == 0:
                    gpad[w, pl.ds(HALF * q_count, seq), :] = low
                else:
                    gpad[w, pl.ds(margin, seq), :] = low
                tra[:, rows_of(w)] = low.T

        def conv_grad(b, group):
            @pl.loop(group[0], group[0] + group[1])
            def _(k):
                part = dot(tra[...], tap(b, k))
                big[slot(b), k] = part.astype(BF).reshape(mp, group_rows, width)

        def in_grad(b, batch=None):
            span = COLS // group_rows
            rows = part_rows(batch)

            @pl.loop(0, width // COLS)
            def _(n):
                total = None
                for k in range(KERNEL):
                    wk = big[b, k, pl.ds(n * span, span)].reshape(COLS, width)
                    term = dot_nt(gtap(b, KERNEL - 1 - k, batch), wk)
                    total = term if total is None else total + term
                acc[rows, cols_of(n)] = total

        def in_back(b, batch):
            x = x0 if b == 0 else x1

            @pl.loop(*part_windows(batch))
            def _(w):
                gn = acc[rows_of(w), :]
                hat, r = norm_parts(x[w].astype(F32))
                gbuf[0, b, 0:1, :] += jnp.sum(gn * hat, axis=0, keepdims=True)
                value = mid[w] + norm_back(gn * gains[b, 0], hat, r)
                if b == 0:
                    x0[w] = from_phases(value).astype(BF)
                else:
                    ig1[w] = value.astype(BF)

                    def keep(r_, tile):
                        gout[w, pl.ds(r_ * q_count, q_count), :] = tile.astype(BF)
                    to_phases(value, keep)

        order = list(range(levels - 1, -1, -1))

        def region(ref, lead, kept, at):
            r0, rn, c0, cn = 0, half_rows, 0, width
            for j in range(levels - 1, kept - 1, -1):
                side = (at // (1 << j)) % 2
                if j >= 2:
                    cn //= 2
                    c0 = c0 + side * cn
                else:
                    rn //= 2
                    r0 = r0 + side * rn
            return r0, rn, c0, cn

        def grad_view(ref, group, half, part):
            j0, nj = group
            r0, rn, c0, cn = part
            rows = pl.ds(pl.multiple_of(half * half_rows + r0, TILE), rn)
            cols = slice(None) if cn == width else pl.ds(pl.multiple_of(c0, 128), cn)
            return ref.at[pl.ds(j0, nj), :, rows, cols]

        def add_into(group, half, part, other):
            j0, nj = group
            r0, rn, c0, cn = part
            rows = pl.ds(pl.multiple_of(half * half_rows + r0, TILE), rn)
            cols = slice(None) if cn == width else pl.ds(pl.multiple_of(c0, 128), cn)
            return j0, nj, rows, cols

        def accumulate(b, group, part, src):
            j0, nj, rows, cols = add_into(group, s, part, src)

            @pl.loop(j0, j0 + nj)
            def _(j):
                at = (slot(b), j, slice(None), rows, cols)
                big[at] = big[at] + src[j]

        def need_credit(n, which):
            if ggroups[n][0] == 0:
                pl.semaphore_wait(credit.at[n % per_grad, which], 1)

        def give_credit(n, which, device):
            if ggroups[n][0] == 1:
                pl.semaphore_signal(credit.at[n % per_grad, which], inc=1, device_id=device, device_id_type=MESH)

        def c_send(n):
            b, group = ggroups[n]
            need_credit(n, 0)
            src = grad_view(big.at[slot(b)], group, 1 - s, (0, half_rows, 0, width))
            begin(rcopy(src, recv_c.at[pl.ds(group[0], group[1])], rc_s.at[n], rc_r.at[n], sibling), None, n)

        def x_exchange(n, i):
            b, group = ggroups[n]
            j0, nj = group
            if i == 0:
                received(recv_c.at[pl.ds(j0, nj)], rc_r.at[n])
                accumulate(b, group, (0, half_rows, 0, width), recv_c)
                give_credit(n, 0, sibling)
            else:
                done = order[i - 1]
                received(recv_x[i - 1].at[pl.ds(j0, nj)], rx_r.at[n, i - 1])
                accumulate(b, group, region(None, None, done, place), recv_x[i - 1])
                give_credit(n, i, partner(done))
            if i < levels:
                j = order[i]
                need_credit(n, 1 + i)
                flip = place + (1 << j) - 2 * (1 << j) * bit(j)
                src = grad_view(big.at[slot(b)], group, s, region(None, None, j, flip))
                begin(rcopy(src, recv_x[i].at[pl.ds(j0, nj)], rx_s.at[n, i], rx_r.at[n, i], partner(j)), None, n)
            else:
                final = region(None, None, 0, place)
                for k in range(1, mp):
                    if n - per_grad not in z_first:
                        need_credit(n, levels + k)
                    rcopy(z_part(b, group, final, peer(k)), recv_z.at[k - 1, pl.ds(j0, nj)],
                          rz_s.at[n], rz_r.at[n], dev(s, peer(k), d)).start()
                held = recv_z.at[:, pl.ds(j0, nj)]
                sends.append((rcopy(held, held, rz_s.at[n], rz_r.at[n], sibling), None, n))

        def z_part(b, group, part, mm):
            j0, nj = group
            r0, rn, c0, cn = part
            rows = pl.ds(pl.multiple_of(s * half_rows + r0, TILE), rn)
            cols = slice(None) if cn == width else pl.ds(pl.multiple_of(c0, 128), cn)
            if j0 < KERNEL:
                return big.at[slot(b), pl.ds(j0, nj), mm, rows, cols]
            return big.at[slot(b), j0 + mm, :, rows, cols]

        def finish(n):
            b, group = ggroups[n]
            j0, nj = group
            final = region(None, None, 0, place)
            r0, rn, c0, cn = final
            received(recv_z.at[:, pl.ds(j0, nj)], rz_r.at[n])
            total = z_part(b, group, final, m)[...].astype(F32)
            for k in range(1, mp):
                total = total + recv_z[k - 1, pl.ds(j0, nj)].astype(F32)
            if n + per_grad not in z_first:
                for k in range(1, mp):
                    give_credit(n, levels + k, dev(s, peer(mp - k), d))
            piece[b, pl.ds(j0, nj)] = total.astype(BF)
            spread(n)

        def spread(n):
            b, group = ggroups[n]
            j0, nj = group
            r0, rn, c0, cn = region(None, None, 0, place)
            rows = pl.ds(pl.multiple_of(s * half_rows + r0, TILE), rn)
            cols = slice(None) if cn == width else pl.ds(pl.multiple_of(c0, 128), cn)
            dst = fin.at[pl.ds(j0, nj), rows, cols]
            src = piece.at[b, pl.ds(j0, nj)]

            pl.when(s == b)(pltpu.make_async_copy(src, dst, rf_r.at[0]).start)
            begin(rcopy(src, dst, rf_s.at[n, 0], rf_r.at[0], sibling), s != b, n)
            for o in range(1, dp):
                begin(rcopy(src, dst, rf_s.at[n, o], rf_r.at[0], dev(b, m, across(o))), None, n)

        def shard_part(n, mm, part):
            b, (j0, nj) = ggroups[n]
            r0, rn, c0, cn = part
            rows = pl.ds(pl.multiple_of(s * half_rows + r0, TILE), rn)
            cols = slice(None) if cn == width else pl.ds(pl.multiple_of(c0, 128), cn)
            if j0 < KERNEL:
                return (slot(b), pl.ds(j0, nj), mm, rows, cols)
            return (slot(b), j0 + mm, slice(None), rows, cols)

        side = (0, half_rows, 0, width)

        def z_pair(stage):
            if stage == 0:
                other = m + 1 - 2 * lax.rem(m, 2)
                return other, [(lax.rem(other, 2) + 2 * i, lax.rem(m, 2) + 2 * i, i) for i in range(2)]
            other = m + 2 - 4 * (m // 2)
            return other, [(other, m, 2)]

        def z_landing(n, i):
            return recv_zf.at[z_first[n], i, pl.ds(0, ggroups[n][1][1])]

        def z_first_send(n, stage):
            other, parts = z_pair(stage)
            at = z_order.index(n)
            for theirs, _, i in parts:
                begin(rcopy(big.at[shard_part(n, theirs, side)], z_landing(n, i),
                            zf_s.at[at, i], zf_r.at[at, i], dev(s, other, d)), None, n)

        def z_first_take(n, stage):
            other, parts = z_pair(stage)
            at = z_order.index(n)
            for _, mine, i in parts:
                received(z_landing(n, i), zf_r.at[at, i])
                where = shard_part(n, mine, side)
                big[where] = big[where] + recv_zf[z_first[n], i, pl.ds(0, ggroups[n][1][1])]

        def z_first_cross(n, i):
            j0, nj = ggroups[n][1]
            if i:
                done = order[i - 1]
                received(recv_x[i - 1].at[j0, pl.ds(0, nj)], rx_r.at[n, i - 1])
                where = shard_part(n, m, region(None, None, done, place))
                big[where] = big[where] + recv_x[i - 1][j0, pl.ds(0, nj)]
                give_credit(n, i, partner(done))
            if i < levels:
                j = order[i]
                need_credit(n, 1 + i)
                flip = place + (1 << j) - 2 * (1 << j) * bit(j)
                begin(rcopy(big.at[shard_part(n, m, region(None, None, j, flip))], recv_x[i].at[j0, pl.ds(0, nj)],
                            rx_s.at[n, i], rx_r.at[n, i], partner(j)), None, n)

        def z_first_chain(n):
            b, group = ggroups[n]
            j0, nj = group
            size = nj * width * width * 2 / 1e3
            c_send(n)
            yield post("core", size / 2, 500)
            received(recv_c.at[pl.ds(j0, nj)], rc_r.at[n])
            accumulate(b, group, side, recv_c)
            give_credit(n, 0, sibling)
            for stage in range(2):
                z_first_send(n, stage)
                yield post("z", size / 4 / (1 + stage), 50)
                z_first_take(n, stage)
            for i in range(levels):
                z_first_cross(n, i)
                yield post("xy", size / 16 / (1 << i), 100)
            z_first_cross(n, levels)
            piece[b, pl.ds(j0, nj)] = big[shard_part(n, m, region(None, None, 0, place))]
            spread(n)
            post("xy", size / 2 / dp / mp * dp / 2, 100)

        def across(o):
            out = d
            for j in range(levels):
                if (o >> j) & 1:
                    out = out + (1 << j) - 2 * (1 << j) * ((d // (1 << j)) % 2)
            return out

        def reduce_chain(n):
            if n in z_first:
                yield from z_first_chain(n)
                return
            b, group = ggroups[n]
            size = group[1] * width * width * 2 / 1e3
            c_send(n)
            yield post("core", size / 2, 500)
            for i in range(levels):
                x_exchange(n, i)
                yield post("xy", size / 4 / (1 << i), 100)
            x_exchange(n, levels)
            yield post("z", 2 * size / 2 / dp, 100)
            finish(n)
            post("xy", size / 2 / dp / mp * dp / 2, 100)

        first, second = range(per_block), range(per_block, 2 * per_block)
        for copy in loads:
            copy.wait()
        gbuf[0] = jnp.zeros((2, 8, width), F32)
        received(gains.at[1 - s, 0], gn_r.at[0])
        received(gains.at[1 - s, 1], gn_r.at[levels + mp])
        work(2.5, first_norm, 0)
        stage_edges(xext)
        arrived = halo_send(0)
        for n in range(1, per_block):
            begin_gather(n)
        halo_wait(0, 0, arrived)
        work(0.5, fill_edges, xext)
        for g in range(3):
            complete([(0, g)])
            for n in range(width // COLS):
                work(1.0, conv_part, 0, range(3 * g, 3 * g + 3), None, n)
        for batch in range(batches):
            work(1.0, middle, 0, batch)
        complete([(0, 3)])
        for quarter in range(4):
            work(1.0, up, 0, None, quarter, 4)
        spill = [pltpu.make_async_copy(hid, sp_hid, loc.at[4]), pltpu.make_async_copy(slo, sp_slo, loc.at[5])]
        for copy in spill:
            copy.start()
        complete([(0, 4)])
        arrived = []
        for batch in range(batches):
            work(0.7, down, 0, batch)
            work(1.3, down_out, 0, batch)
            work(0.7, first_norm, 1, batch)
            arrived.append(halo_send(1, batch))
        send_home(x1, blk, 0, 0)
        zero_edges(xpad)
        zero_edges(gpad)
        work(2.5, branch_grad, 1)
        for batch in range(batches):
            halo_wait(1, batch, arrived[batch])
            if batch == 0:
                complete([(0, per_block + g) for g in range(3)])
            for n in range(width // COLS):
                work(1.0, conv_part, 1, range(KERNEL), batch, n)
            work(1.0, middle, 1, batch)
            if batch == 0:
                for copy in spill:
                    copy.wait()
                complete([(0, per_block + 3)])
            for half in range(2):
                work(0.7, up, 1, batch, half, 2)
        work(2.2, down_grad, 1)
        launch((1, 0), reduce_chain(0))
        work(1.5, transposed_ffn, 1)
        complete([(0, per_block + 4)])
        work(3.0, pre_grad, 1)
        work(2.2, up_grad, 1)
        launch((1, 1), reduce_chain(1))
        work(2.5, ffn_grad, 1)
        arrived = []
        for batch in range(batches):
            work(1.2, ffn_back, 1, batch)
            arrived.append(halo_send(3, batch))
        for g, group in enumerate(back_groups):
            work(0.7 * group[1], conv_grad, 1, group)
            launch((1, 2 + g), reduce_chain(2 + g))
        work(2.0, down, 1, None)
        work(1.0, down_out, 1, None)
        send_home(x2, blk, 1, 1)
        fetch = [pltpu.make_async_copy(sp_hid, hid, loc.at[6]), pltpu.make_async_copy(sp_slo, slo, loc.at[7])]
        for copy in fetch:
            copy.start()
        for batch in range(batches):
            halo_wait(3, batch, arrived[batch])
            work(1.8, in_grad, 1, batch)
            work(1.0, in_back, 1, batch)
        send_home(ig1, ing, 1, 3)
        flush(("gather", 1))
        work(2.5, branch_grad, 0)
        for copy in fetch:
            copy.wait()
        work(2.2, down_grad, 0)
        launch((1, per_grad), reduce_chain(per_grad))
        work(1.5, transposed_ffn, 0)
        work(3.0, pre_grad, 0)
        work(2.2, up_grad, 0)
        launch((1, per_grad + 1), reduce_chain(per_grad + 1))
        flush("halo")
        work(2.5, ffn_grad, 0)
        for batch in range(batches):
            work(1.2, ffn_back, 0, batch)
        stage_edges(gpad)
        arrived = halo_send(2)
        for g, group in enumerate(back_groups):
            work(0.7 * group[1], conv_grad, 0, group)
            launch((1, per_grad + 2 + g), reduce_chain(per_grad + 2 + g))
        halo_wait(2, 0, arrived)
        work(0.5, fill_edges, gpad)
        work(5.0, in_grad, 0)
        for batch in range(batches):
            work(1.0, in_back, 0, batch)
        send_home(x0, ing, 0, 2)

        def gain_chain():
            begin(rcopy(gbuf.at[0], grecv.at[0], gn_s.at[1], gn_r.at[1], sibling))
            for i in range(levels + 1):
                yield clock["now"] + LATENCY
                received(grecv.at[i], gn_r.at[1 + i])
                gbuf[i + 1] = gbuf[i] + grecv[i]
                if i < levels:
                    begin(rcopy(gbuf.at[i + 1], grecv.at[i + 1], gn_s.at[2 + i], gn_r.at[2 + i], partner(i)))
            for k in range(1, mp):
                at = levels + k
                begin(rcopy(gbuf.at[levels + 1], grecv.at[at], gn_s.at[1 + at], gn_r.at[1 + at], dev(s, peer(k), d)))
            yield clock["now"] + 2 * LATENCY
            total = gbuf[levels + 1]
            for k in range(1, mp):
                at = levels + k
                received(grecv.at[at], gn_r.at[1 + at])
                total = total + grecv[at]
            gbuf[levels + 2] = total

        launch((2, 0), gain_chain())
        for n in range(nwg):
            z_flush(n)
        flush(("gather", 0))
        flush("halo")
        for n in range(ngg):
            if (1, n) not in chains:
                flush(n)
        complete(list(chains))
        out = pltpu.make_async_copy(
            gbuf.at[levels + 2, s, :, pl.ds(pl.multiple_of(m * group_rows, group_rows), group_rows)], gout_sum, loc.at[0])
        out.start()
        received(fin, rf_r.at[0])
        flush()
        sent_home(x1, blk, 0, 0)
        sent_home(x2, blk, 1, 1)
        sent_home(x0, ing, 0, 2)
        sent_home(ig1, ing, 1, 3)
        out.wait()

    vm = pltpu.VMEM
    dma = pltpu.SemaphoreType.DMA
    plain = (nw, seq, width)
    flat = (rows_all, width)

    def recv_shape(i):
        r, c = half_rows, width
        for j in range(levels - 1, levels - 2 - i, -1):
            if j >= 2:
                c //= 2
            else:
                r //= 2
        return (nblk, mp, r, c)

    piece_shape = (nblk, recv_shape(levels - 1)[2], recv_shape(levels - 1)[3])
    scratch = [
        vm((3, nblk, mp, group_rows, width), BF),
        vm((nblk, mp, half_rows, width), BF),
        vm((mp - 1,) + piece_shape, BF),
        vm((max(1, min(2, len(Z_FIRST))), 3, mp, half_rows, width), BF),
        vm((2,) + piece_shape, BF),
        vm((nw, 2 * seq, width), BF),
        vm((nw, 2 * margin + seq, width), BF),
        vm((nw, 2 * margin + seq, width), BF),
        vm((rows_all, mp * width), BF),
        vm((rows_all, mp * width), BF),
        vm(plain, BF),
        vm(plain, BF),
        vm(plain, BF),
        vm((2,) + plain, BF),
        vm((2,) + flat, BF),
        vm((2,) + plain, BF),
        vm(plain, BF),
        vm(flat, BF),
        vm((width, rows_all), BF),
        vm((width, rows_all), BF),
        vm(flat, F32),
        vm(plain, F32),
        vm(plain, BF),
        vm((2, 2, 1, width), F32),
        vm((width // 128, seq, 128), F32),
        vm((2 * HALF, q_count + 16, width), F32),
        vm((2, nw, 8, width), F32),
        vm((2, nw, 8, width), F32),
        vm((levels + 3, 2, 8, width), F32),
        vm((levels + mp, 2, 8, width), F32),
    ] + [vm(recv_shape(i), BF) for i in range(levels)] + [
        dma((per_block, mp - 1, 2)), dma((nwg, mp - 1)), dma((nwg,)),
        dma((nwg, levels)), dma((nwg, levels)),
        dma((nwg,)), dma((nwg,)),
        dma((per_block,)), dma((per_block,)), dma((per_block,)),
        dma((ngg,)), dma((ngg,)),
        dma((ngg, levels)), dma((ngg, levels)),
        dma((ngg,)), dma((ngg,)),
        dma((1 + len(z_first), 3)), dma((1 + len(z_first), 3)),
        dma((ngg, dp)), dma((1,)),
        dma((1 + levels + mp + 1,)), dma((1 + levels + mp + 1,)),
        dma((4, batches, 2)), dma((4, batches, 2)),
        dma((4,)), dma((4,)),
        dma((8,)),
        pltpu.SemaphoreType.REGULAR((per_grad, levels + mp)),
    ]
    return body, scratch


def per_device(tokens, valid, conv_weight, gain_one, gain_two, up_weight, down_weight, cotangent):
    mp = lax.axis_size("mp")
    dp = lax.axis_size("dp")
    windows, seq, width = tokens.shape
    nw = windows // 2
    rows = width // mp
    body, scratch = make_kernel(mp, dp, nw, seq, width)
    conv = conv_weight[0].reshape(KERNEL, mp, rows, rows)
    up = up_weight[0].reshape(mp, rows, width)
    down = down_weight[0].reshape(mp, rows, width)
    nblk = KERNEL + 2 * mp
    anywhere = pl.BlockSpec(memory_space=pl.ANY)
    blk, ing, fin, sums, _, _ = pl.pallas_call(
        body,
        out_shape=(
            jax.ShapeDtypeStruct(tokens.shape, BF),
            jax.ShapeDtypeStruct(tokens.shape, BF),
            jax.ShapeDtypeStruct((nblk, rows, width), BF),
            jax.ShapeDtypeStruct((8, rows), F32),
            jax.ShapeDtypeStruct((nw * seq, mp * width), BF),
            jax.ShapeDtypeStruct((nw * seq, mp * width), BF),
        ),
        in_specs=[anywhere] * 2 + [pl.BlockSpec(memory_space=pltpu.SMEM)] + [anywhere] * 5,
        out_specs=[anywhere] * 6,
        scratch_shapes=scratch,
        compiler_params=pltpu.CompilerParams(
            collective_id=0, has_side_effects=True, vmem_limit_bytes=64 * 1024 * 1024 - 64 * 1024
        ),
    )(tokens, cotangent, valid, gain_one, gain_two, conv, up, down)
    return finalize(mp, blk, ing, fin, sums)


def finalize(mp, blk, ing, fin, sums):
    nblk, rows, width = fin.shape

    def body(blk_in, ing_in, fin_in, sums_in, blk_out, ing_out, conv_out, one_out, two_out, up_out, down_out,
             held, conv, up, down, acts, sem):
        moves = [pltpu.make_async_copy(blk_in, acts.at[0], sem.at[0]),
                 pltpu.make_async_copy(ing_in, acts.at[1], sem.at[1])]
        parts = [(0, KERNEL), (KERNEL, mp), (KERNEL + mp, mp)]
        reads = [pltpu.make_async_copy(fin_in.at[pl.ds(a, n)], held.at[pl.ds(a, n)], sem.at[2 + i])
                 for i, (a, n) in enumerate(parts)]
        for copy in moves + reads:
            copy.start()
        one_out[...] = sums_in[0:1, :]
        two_out[...] = sums_in[1:2, :]
        writes = []

        def store(src, dst, at):
            copy = pltpu.make_async_copy(src, dst, sem.at[at])
            copy.start()
            writes.append(copy)

        for i, out in enumerate((blk_out, ing_out)):
            moves[i].wait()
            store(acts.at[i], out.at[0], 10 + i)
        reads[0].wait()
        for k in range(KERNEL):
            conv[k] = held[k].astype(F32).T
            if k % 3 == 2:
                store(conv.at[pl.ds(k - 2, 3)], conv_out.at[0, pl.ds(k - 2, 3)], 5 + k // 3)
        reads[2].wait()
        for j in range(mp):
            down[:, j * rows:(j + 1) * rows] = held[KERNEL + mp + j].astype(F32).T
        store(down, down_out.at[0], 8)
        reads[1].wait()
        for j in range(mp):
            up[j * rows:(j + 1) * rows, :] = held[KERNEL + j].astype(F32)
        store(up, up_out.at[0], 9)
        for copy in writes:
            copy.wait()

    anywhere = pl.BlockSpec(memory_space=pl.ANY)
    vmem = pl.BlockSpec(memory_space=pltpu.VMEM)
    square = (mp * rows, width)
    return pl.pallas_call(
        body,
        out_shape=(
            jax.ShapeDtypeStruct((1,) + blk.shape, BF),
            jax.ShapeDtypeStruct((1,) + ing.shape, BF),
            jax.ShapeDtypeStruct((1, KERNEL, width, rows), F32),
            jax.ShapeDtypeStruct((1, rows), F32),
            jax.ShapeDtypeStruct((1, rows), F32),
            jax.ShapeDtypeStruct((1,) + square, F32),
            jax.ShapeDtypeStruct((1, width, mp * rows), F32),
        ),
        in_specs=[anywhere, anywhere, anywhere, vmem],
        out_specs=[anywhere, anywhere, anywhere, vmem, vmem, anywhere, anywhere],
        scratch_shapes=[
            pltpu.VMEM(fin.shape, BF),
            pltpu.VMEM((KERNEL, width, rows), F32),
            pltpu.VMEM(square, F32),
            pltpu.VMEM((width, mp * rows), F32),
            pltpu.VMEM((2,) + blk.shape, BF),
            pltpu.SemaphoreType.DMA((12,)),
        ],
        compiler_params=pltpu.CompilerParams(vmem_limit_bytes=64 * 1024 * 1024 - 64 * 1024),
    )(blk, ing, fin, sums)


def solution(mesh):
    in_specs = (
        P("dp", "mp", None),
        P("dp"),
        P("section", None, None, "mp"),
        P("section", None),
        P("section", None),
        P("section", None, "mp"),
        P("section", "mp", None),
        P("dp", "mp", None),
    )
    out_specs = (
        P("section", "dp", "mp", None),
        P("section", "dp", "mp", None),
        P("section", None, None, "mp"),
        P("section", "mp"),
        P("section", "mp"),
        P("section", None, "mp"),
        P("section", "mp", None),
    )
    return jax.shard_map(
        per_device, mesh=mesh, in_specs=in_specs, out_specs=out_specs, check_vma=False
    )
```

```python
import jax
import jax.numpy as jnp
from jax import lax
from jax.experimental import pallas as pl
from jax.experimental.pallas import tpu as pltpu
from jax.sharding import PartitionSpec as P

KERNEL = 9
DILATION = 32
HALF = KERNEL // 2
PHASES = 8
TILE = 16
COLS = 256
C0 = 0.7978845608028654
C1 = 0.044715
BF = jnp.bfloat16
F32 = jnp.float32
MESH = pl.DeviceIdType.MESH
LATENCY = 2.0
NEVER = 1e9
WIDE_Z = 0
AHEAD = 1.0
Z_FIRST = (7,)


def gelu_and_slope(v):
    v2 = v * v
    h = 0.5 + 0.5 * jnp.tanh(v * (C0 + (C0 * C1) * v2))
    out = v * h
    return out, h + out * (1.0 - h) * (2.0 * C0 + (6.0 * C0 * C1) * v2)


def norm_parts(values):
    center = values - jnp.mean(values, axis=-1, keepdims=True)
    r = lax.rsqrt(jnp.mean(center * center, axis=-1, keepdims=True) + 1e-05)
    return center * r, r


def norm_back(g, hat, r):
    return r * (
        g
        - jnp.mean(g, axis=-1, keepdims=True)
        - hat * jnp.mean(g * hat, axis=-1, keepdims=True)
    )


def dot(a, b):
    return jnp.dot(a, b, preferred_element_type=F32)


def dot_nt(a, b):
    return lax.dot_general(a, b, (((1,), (1,)), ((), ())), preferred_element_type=F32)


def make_kernel(mp, dp, nw, seq, width):
    levels = dp.bit_length() - 1
    assert dp == 1 << levels and 2 <= levels <= 4
    rows_all = nw * seq
    q_count = seq // PHASES
    group_rows = width // mp
    half_rows = group_rows // 2
    nblk = KERNEL + 2 * mp
    margin = HALF * DILATION
    conv_groups = [(0, 3), (3, 3), (6, 3)]
    wgroups = [(b, g) for b in range(2) for g in conv_groups + [(KERNEL, mp), (KERNEL + mp, mp)]]
    back_groups = [(0, 3), (3, 3), (6, 2), (8, 1)]
    ggroups = [(b, g) for b in (1, 0) for g in [(KERNEL + mp, mp), (KERNEL, mp)] + back_groups]
    per_grad = len(back_groups) + 2
    z_order = list(Z_FIRST)
    assert len(z_order) <= 2
    z_first = {g: i % 2 for i, g in enumerate(z_order)}
    batches = 2 if nw % 2 == 0 else 1
    wb = nw // batches
    nwg, ngg = len(wgroups), len(ggroups)
    per_block = len(conv_groups) + 2
    piece_cols = width if levels == 2 else width >> (levels - 2)

    def body(tok, cot, valid, one_in, two_in, conv_in, up_in, down_in,
             blk, ing, fin, gout_sum, sp_hid, sp_slo,
             big, recv_c, recv_z, recv_zf, piece, xext, xpad, gpad, hid, slo, x0, x1, x2, midb, ffn,
             slope1, gout, gb, tra, trb, acc, mid, ig1, gains, slab, edge, hsend, hrecv,
             gbuf, grecv, gz, *rest):
        recv_x = rest[:levels]
        (agz_s, agz_r, agf_s, agx_s, agx_r, agk_s, agk_r, own_l, own_s, own_r, rc_s, rc_r, rx_s, rx_r,
         rz_s, rz_r, zf_s, zf_r, rf_s, rf_r, gn_s, gn_r, halo_s, halo_r, out_s, out_r, loc, credit) = rest[levels:]
        s = lax.axis_index("section")
        m = lax.axis_index("mp")
        d = lax.axis_index("dp")

        def dev(ss, mm, dd):
            return {"section": ss, "mp": mm, "dp": dd}

        sibling = dev(1 - s, m, d)

        flipped = 0
        for j in range(levels):
            flipped = flipped + ((d // (1 << j)) % 2) * (1 << (levels - 1 - j))
        place = (1 - s) * d + s * flipped

        def bit(j):
            return (place // (1 << j)) % 2

        def partner(j):
            other = (1 - s) * (1 << j) + s * (1 << (levels - 1 - j))
            has = (d // other) % 2
            return dev(s, m, d + other - 2 * other * has)

        def peer(k):
            return lax.rem(m + k, mp)

        def rcopy(src, dst, ssem, rsem, device):
            return pltpu.make_async_remote_copy(
                src_ref=src, dst_ref=dst, send_sem=ssem, recv_sem=rsem,
                device_id=device, device_id_type=MESH)

        sends = []

        def begin(copy, cond=None, kind=None):
            if cond is None:
                copy.start()
            else:
                pl.when(cond)(copy.start)
            sends.append((copy, cond, kind))

        def flush(kind=None):
            for copy, cond, its in [x for x in sends if kind is None or x[2] == kind]:
                if cond is None:
                    copy.wait_send()
                else:
                    pl.when(cond)(copy.wait_send)
            sends[:] = [x for x in sends if kind is not None and x[2] != kind]

        barrier = pltpu.get_barrier_semaphore()
        count = 0
        for o in range(dp):
            for ss in range(2):
                if o == 0 and ss == 0:
                    continue
                other = d + o - dp * ((d + o) // dp)
                pl.semaphore_signal(
                    barrier, inc=1, device_id=dev(s + ss - 2 * s * ss, m, other), device_id_type=MESH)
                count += 1
        for k in range(1, mp):
            for ss in range(2):
                pl.semaphore_signal(
                    barrier, inc=1, device_id=dev(s + ss - 2 * s * ss, peer(k), d), device_id_type=MESH)
                count += 1
        loads = [
            pltpu.make_async_copy(tok.at[pl.ds(s * nw, nw)], x1, loc.at[0]),
            pltpu.make_async_copy(one_in, gains.at[s, 0], loc.at[1]),
            pltpu.make_async_copy(two_in, gains.at[s, 1], loc.at[2]),
            pltpu.make_async_copy(cot.at[pl.ds(s * nw, nw)], gout, loc.at[3]),
        ]
        for copy in loads:
            copy.start()
        pl.semaphore_wait(barrier, count)

        def shard_view(b, group, mm):
            j0, nj = group
            if j0 < KERNEL:
                return big.at[b, pl.ds(j0, nj), :, :, pl.ds(pl.multiple_of(mm * group_rows, group_rows), group_rows)]
            return big.at[b, j0 + mm]

        def own_source(group):
            j0, nj = group
            if j0 < KERNEL:
                return conv_in.at[pl.ds(j0, nj)]
            return up_in if j0 == KERNEL else down_in

        def sub(ref, half, at, level):
            lead = ref.shape[:-3]
            idx = (slice(None),) * len(lead)
            step = half_rows // min(dp, 4)
            if levels == 2:
                first = ((at // (1 << level)) * (1 << level)) * step
                return ref.at[idx + (slice(None), pl.ds(pl.multiple_of(half * half_rows + first, TILE), step << level))]
            low, high = at % 4, at // 4
            if level <= 2:
                first = ((low // (1 << level)) * (1 << level)) * step
                return ref.at[idx + (pl.ds(high, 1), pl.ds(pl.multiple_of(half * half_rows + first, TILE), step << level))]
            up = level - 2
            first = (high // (1 << up)) * (1 << up)
            return ref.at[idx + (pl.ds(first, 1 << up), pl.ds(pl.multiple_of(half * half_rows, TILE), half_rows))]

        def place_of(half):
            return d if half == 0 else flipped

        own = []
        for i, group in enumerate(conv_groups + [(KERNEL, mp), (KERNEL + mp, mp)]):
            src, dst = own_source(group), shard_view(s, group, m)
            local = pltpu.make_async_copy(src, dst, own_l.at[i])
            local.start()
            own.append(local)
        begin(rcopy(one_in, gains.at[s, 0], gn_s.at[0], gn_r.at[0], sibling))
        begin(rcopy(two_in, gains.at[s, 1], gn_s.at[1], gn_r.at[1], sibling))

        def z_level(n):
            b, group = wgroups[n]
            return WIDE_Z if b == 1 and group[0] >= KERNEL and levels == 2 else 0

        def z_copies(n):
            b, group = wgroups[n]
            i = n % per_block
            out = [(rcopy(own_source(group), shard_view(b, group, m), own_s.at[i], own_r.at[i], sibling), None)]
            for k in (2, 1, 3):
                for half in range(2):
                    copy = rcopy(
                        sub(own_source(group), half, place_of(half), z_level(n)),
                        sub(shard_view(b, group, m), half, place_of(half), z_level(n)),
                        agz_s.at[i, k - 1, half], agz_r.at[n, k - 1], dev(half, peer(k), d))
                    out.append((copy, None if k == 2 else (m != 3 if k == 1 else m != 0)))
            return out

        def z_send(n):
            @pl.when(s == wgroups[n][0])
            def _():
                for copy, cond in z_copies(n):
                    if cond is None:
                        copy.start()
                    else:
                        pl.when(cond)(copy.start)

        def z_flush(n):
            @pl.when(s == wgroups[n][0])
            def _():
                for copy, cond in z_copies(n):
                    if cond is None:
                        copy.wait_send()
                    else:
                        pl.when(cond)(copy.wait_send)

        def received(dst, rsem):
            rcopy(dst, dst, rsem, rsem, sibling).wait_recv()

        def z_forward(n):
            b, group = wgroups[n]
            held = sub(shard_view(b, group, peer(mp - 2)), s, place, z_level(n))
            received(held, agz_r.at[n, 1])
            for at, to, k in ((2, 3, 3), (1, 0, 1)):
                begin(rcopy(held, held, agf_s.at[n], agz_r.at[n, k - 1], dev(s, to, d)), m == at, ("gather", b))

        def run_view(b, group, first, count):
            j0, nj = group
            if j0 < KERNEL:
                return big.at[b, pl.ds(j0, nj), :, :, pl.ds(first * group_rows, count * group_rows)]
            return big.at[b, pl.ds(j0 + first, count)]

        def foreign(n, half, at, level):
            b, group = wgroups[n]
            return sub(run_view(b, group, 0, mp - 1), half, at, level)

        def x_step(n, level):
            b, group = wgroups[n]
            if level == z_level(n):
                for k in (1, 3):
                    received(sub(shard_view(b, group, peer(mp - k)), s, place, level), agz_r.at[n, k - 1])
            else:
                received(foreign(n, s, place, level - 1), agx_r.at[n, level - 1])
            if level < levels:
                sems, to = (agx_s.at[n, level], agx_r.at[n, level]), partner(level)
            else:
                sems, to = (agk_s.at[n], agk_r.at[n]), sibling
            for mine in range(mp):
                @pl.when(m == mine)
                def _():
                    for first, count in ((0, mine), (mine + 1, mp - 1 - mine)):
                        if count:
                            part = sub(run_view(b, group, first, count), s, place, level)
                            rcopy(part, part, *sems, to).start()
            held = foreign(n, s, place, level)
            sends.append((rcopy(held, held, *sems, to), None, ("gather", b)))

        def gathered(n):
            b, group = wgroups[n]
            i = n % per_block

            @pl.when(s == b)
            def _():
                pltpu.make_async_copy(own_source(group), shard_view(b, group, m), own_l.at[i]).wait()

            @pl.when(s != b)
            def _():
                received(shard_view(b, group, m), own_r.at[i])

            received(foreign(n, 1 - s, 0, levels), agk_r.at[n])

        clock = {"now": 4.0}
        gate = {"open": False}
        busy = {}
        chains = {}

        def post(link, size, rate):
            start = max(clock["now"], busy.get(link, 0.0))
            busy[link] = start + size / rate
            return busy[link] + LATENCY

        def resume(key):
            try:
                chains[key][0] = next(chains[key][1])
            except StopIteration:
                del chains[key]

        def launch(key, chain):
            chains[key] = [0.0, chain]
            resume(key)

        def service():
            while True:
                ready = [(c[0], key) for key, c in chains.items()
                         if c[0] <= clock["now"] + (AHEAD if key[0] == 0 and key[1] < per_block else 0.0)]
                if not ready:
                    return
                when, key = min(ready)
                clock["now"] = max(clock["now"], when)
                resume(key)

        def complete(keys):
            while any(key in chains for key in keys):
                when, key = min((c[0], key) for key, c in chains.items())
                clock["now"] = max(clock["now"], when)
                resume(key)

        def work(cost, call, *args):
            call(*args)
            clock["now"] += cost
            service()

        def gather_chain(n):
            b, group = wgroups[n]
            unit = (group[1] * width * group_rows if group[0] < KERNEL else width * width) * 2 / (2 * dp) / 1e3
            yield post("z", 6 * unit * (1 << z_level(n)), 100)
            if n == per_block - 2:
                for later in range(per_block, nwg):
                    begin_gather(later)
            if b == 1 and not gate["open"]:
                yield NEVER
            z_forward(n)
            yield clock["now"] + LATENCY
            for level in range(z_level(n), levels):
                if level > z_level(n):
                    yield when
                x_step(n, level)
                when = post("xy", 3 * unit * (1 << level), 100)
            if n == per_block - 1:
                gate["open"] = True
                for chain in chains.values():
                    if chain[0] == NEVER:
                        chain[0] = clock["now"]
            yield when
            x_step(n, levels)
            yield post("core", 3 * unit * dp, 500)
            gathered(n)

        def begin_gather(n):
            z_send(n)
            launch((0, n), gather_chain(n))

        begin_gather(0)

        def halo_pairs(index, batch):
            if index % 2 == 0:
                up = (hsend.at[0], hrecv.at[0])
                down = (hsend.at[1], hrecv.at[1])
            else:
                ref = xpad if index == 1 else gpad
                part = pl.ds(batch * wb, wb)
                mine = ref.at[part, pl.ds(margin, seq)]
                up = (mine, ref.at[part, pl.ds(0, margin)])
                down = (mine, ref.at[part, pl.ds(margin + seq, margin)])
            return up, down

        def halo_send(index, batch=0):
            up, down = halo_pairs(index, batch)
            begin(rcopy(up[0], up[1], halo_s.at[index, batch, 0], halo_r.at[index, batch, 0],
                        dev(s, lax.rem(m + 1, mp), d)), m < mp - 1, "halo")
            begin(rcopy(down[0], down[1], halo_s.at[index, batch, 1], halo_r.at[index, batch, 1],
                        dev(s, lax.rem(m + mp - 1, mp), d)), m > 0, "halo")
            return post("z", (wb * seq * width * 2 / 1e3) if index % 2 else 98.0, 50)

        def halo_wait(index, batch=0, when=0.0):
            while chains and min(c[0] for c in chains.values()) <= when:
                first, key = min((c[0], key) for key, c in chains.items())
                clock["now"] = max(clock["now"], first)
                resume(key)
            clock["now"] = max(clock["now"], when)
            up, down = halo_pairs(index, batch)
            pl.when(m > 0)(lambda: received(up[1], halo_r.at[index, batch, 0]))
            pl.when(m < mp - 1)(lambda: received(down[1], halo_r.at[index, batch, 1]))

        def zero_edges(ref):
            @pl.when(m == 0)
            def _():
                ref[:, :margin] = jnp.zeros((nw, margin, width), BF)

            @pl.when(m == mp - 1)
            def _():
                ref[:, margin + seq:] = jnp.zeros((nw, margin, width), BF)

        def tile(j):
            return pl.ds(j * q_count, q_count)

        def stage_edges(ext):
            @pl.loop(0, nw)
            def _(w):
                for j in range(HALF):
                    last = ext[w, tile(PHASES + j), :].astype(F32)
                    hsend[0, w, pl.ds(j, 1), :] = last[q_count - 1:, :]
                    first = ext[w, tile(HALF + j), :].astype(F32)
                    hsend[1, w, pl.ds(j, 1), :] = first[:1, :]

        def fill_edges(ext):
            @pl.when(m == 0)
            def _():
                hrecv[0] = jnp.zeros((nw, 8, width), F32)

            @pl.when(m == mp - 1)
            def _():
                hrecv[1] = jnp.zeros((nw, 8, width), F32)

            @pl.loop(0, nw)
            def _(w):
                for j in range(HALF):
                    edge[j, pl.ds(8, q_count), :] = ext[w, tile(PHASES + j), :].astype(F32)
                    edge[j, pl.ds(7, 1), :] = hrecv[0, w, pl.ds(j, 1), :]
                    ext[w, tile(j), :] = edge[j, pl.ds(7, q_count), :].astype(BF)
                    edge[HALF + j, pl.ds(8, q_count), :] = ext[w, tile(HALF + j), :].astype(F32)
                    edge[HALF + j, pl.ds(8 + q_count, 1), :] = hrecv[1, w, pl.ds(j, 1), :]
                    ext[w, tile(HALF + PHASES + j), :] = edge[HALF + j, pl.ds(9, q_count), :].astype(BF)

        def to_phases(value, store):
            for c in range(width // 128):
                slab[c] = value[:, c * 128:(c + 1) * 128]
            for r in range(PHASES):
                store(r, jnp.concatenate(
                    [slab[c, pl.ds(r, q_count, stride=PHASES), :] for c in range(width // 128)], axis=1))

        def from_phases(value):
            for r in range(PHASES):
                for c in range(width // 128):
                    slab[c, pl.ds(r, q_count, stride=PHASES), :] = (
                        value[r * q_count:(r + 1) * q_count, c * 128:(c + 1) * 128])
            return jnp.concatenate([slab[c] for c in range(width // 128)], axis=1)

        def window_mask(w):
            return valid[s * nw + w].astype(F32)

        def shifted(ref, b, k, batch):
            first = k * (q_count if b == 0 else DILATION)
            if not isinstance(k, int):
                first = pl.multiple_of(first, TILE)
            if batch is None:
                return ref[:, pl.ds(first, seq), :].reshape(rows_all, width)
            return ref[pl.ds(batch * wb, wb), pl.ds(first, seq), :].reshape(wb * seq, width)

        def tap(b, k, batch=None):
            return shifted(xext if b == 0 else xpad, b, k, batch)

        def gtap(b, k, batch=None):
            return shifted(gpad, b, k, batch)

        def part_rows(batch):
            return slice(None) if batch is None else pl.ds(batch * wb * seq, wb * seq)

        def part_windows(batch):
            return (0, nw) if batch is None else (batch * wb, (batch + 1) * wb)

        def cols_of(n):
            return pl.ds(pl.multiple_of(n * COLS, COLS), COLS)

        def first_norm(b, batch=None):
            @pl.loop(*part_windows(batch))
            def _(w):
                if b == 0:
                    def keep(r, tile):
                        x0[w, pl.ds(r * q_count, q_count), :] = tile.astype(BF)
                    to_phases(x1[w].astype(F32), keep)
                    x = x0[w]
                else:
                    x = x1[w]
                hat, _r = norm_parts(x.astype(F32))
                n = (hat * gains[b, 0]).astype(BF)
                if b == 0:
                    xext[w, pl.ds(HALF * q_count, seq), :] = n
                else:
                    xpad[w, pl.ds(margin, seq), :] = n

        def conv_part(b, taps, batch, n):
            rows, cols = part_rows(batch), pl.ds(n * COLS, COLS)
            wk = big[b, pl.ds(taps[0], len(taps)), :, :, cols].reshape(len(taps) * width, COLS)
            total = dot(jnp.concatenate([tap(b, k, batch) for k in taps], axis=1), wk)
            if taps[0]:
                total = total + acc[rows, cols]
            acc[rows, cols] = total

        def rows_of(w):
            return pl.ds(pl.multiple_of(w * seq, seq), seq)

        def middle(b, batch=None):
            x = x0 if b == 0 else x1

            @pl.loop(*part_windows(batch))
            def _(w):
                act, slope = gelu_and_slope(acc[rows_of(w), :])
                slope1[b, w] = slope.astype(BF)
                value = x[w].astype(F32) + window_mask(w) * act.astype(BF).astype(F32)
                if b == 0:
                    mid[w] = value
                midb[b, w] = value.astype(BF)
                hat, _r = norm_parts(value)
                ffn[b, rows_of(w), :] = (hat * gains[b, 1]).astype(BF)

        def up(b, batch, quarter, quarters):
            count = mp * width // COLS // quarters
            rows = part_rows(batch)

            @pl.loop(quarter * count, (quarter + 1) * count)
            def _(n):
                per = width // COLS
                wk = big[b, KERNEL + n // per, :, :, cols_of(lax.rem(n, per))].reshape(width, COLS)
                h, slope = gelu_and_slope(dot(ffn[b, rows, :], wk))
                hid[rows, cols_of(n)] = h.astype(BF)
                slo[rows, cols_of(n)] = slope.astype(BF)

        def down(b, batch):
            rows = part_rows(batch)

            @pl.loop(0, width // COLS)
            def _(n):
                wk = big[b, pl.ds(KERNEL + mp, mp), :, :, cols_of(n)].reshape(mp * width, COLS)
                acc[rows, cols_of(n)] = dot(hid[rows, :], wk)

        def down_out(b, batch):
            @pl.loop(*part_windows(batch))
            def _(w):
                branch = window_mask(w) * acc[rows_of(w), :]
                if b == 0:
                    x1[w] = from_phases(mid[w] + branch).astype(BF)
                else:
                    x2[w] = (midb[b, w].astype(F32) + branch).astype(BF)

        def send_home(ref, target, b, index):
            dst = target.at[pl.ds(s * nw, nw)]

            @pl.when(s == b)
            def _():
                pltpu.make_async_copy(ref, dst, out_s.at[index]).start()

            @pl.when(s != b)
            def _():
                rcopy(ref, dst, out_s.at[index], out_r.at[index], sibling).start()

        def sent_home(ref, target, b, index):
            dst = target.at[pl.ds(s * nw, nw)]

            @pl.when(s == b)
            def _():
                pltpu.make_async_copy(ref, dst, out_s.at[index]).wait()
                received(target.at[pl.ds((1 - s) * nw, nw)], out_r.at[index])

            @pl.when(s != b)
            def _():
                rcopy(ref, dst, out_s.at[index], out_r.at[index], sibling).wait_send()

        def slot(b):
            return 2 if b == 1 else 1

        def branch_grad(b):
            @pl.loop(0, nw)
            def _(w):
                value = window_mask(w) * gout[w].astype(F32)
                low = value.astype(BF)
                gb[rows_of(w), :] = low
                tra[:, rows_of(w)] = low.T

        def transposed_ffn(b):
            @pl.loop(0, nw)
            def _(w):
                trb[:, rows_of(w)] = ffn[b, rows_of(w), :].T

        def wide(n):
            return pl.ds(pl.multiple_of(n * width, width), width)

        def down_grad(b):
            @pl.loop(0, mp)
            def _(n):
                part = dot(tra[...], hid[:, wide(n)])
                big[slot(b), KERNEL + mp + n] = part.astype(BF).reshape(mp, group_rows, width)

        def pre_grad(b):
            @pl.loop(0, mp * width // COLS)
            def _(n):
                per = width // COLS
                span = COLS // group_rows
                wk = big[b, KERNEL + mp + n // per, pl.ds(lax.rem(n, per) * span, span)].reshape(COLS, width)
                g = dot_nt(gb[...], wk) * slo[:, cols_of(n)].astype(F32)
                slo[:, cols_of(n)] = g.astype(BF)

        def up_grad(b):
            @pl.loop(0, mp)
            def _(n):
                part = dot(trb[...], slo[:, wide(n)])
                big[slot(b), KERNEL + n] = part.astype(BF).reshape(mp, group_rows, width)

        def ffn_grad(b):
            span = COLS // group_rows

            @pl.loop(0, width // COLS)
            def _(n):
                wk = [big[b, KERNEL + mm, pl.ds(n * span, span)].reshape(COLS, width) for mm in range(mp)]
                acc[:, cols_of(n)] = dot_nt(slo[...], jnp.concatenate(wk, axis=1))

        def ffn_back(b, batch):
            @pl.loop(*part_windows(batch))
            def _(w):
                gf = acc[rows_of(w), :]
                hat, r = norm_parts(midb[b, w].astype(F32))
                gbuf[0, 2 * b + 1:2 * b + 2, :] += jnp.sum(gf * hat, axis=0, keepdims=True)
                gm = gout[w].astype(F32) + norm_back(gf * gains[b, 1], hat, r)
                mid[w] = gm
                ga = (window_mask(w) * gm).astype(BF).astype(F32)
                gc = ga * slope1[b, w].astype(F32)
                low = gc.astype(BF)
                if b == 0:
                    gpad[w, pl.ds(HALF * q_count, seq), :] = low
                else:
                    gpad[w, pl.ds(margin, seq), :] = low
                tra[:, rows_of(w)] = low.T

        def conv_grad(b, group):
            @pl.loop(group[0], group[0] + group[1])
            def _(k):
                part = dot(tra[...], tap(b, k))
                big[slot(b), k] = part.astype(BF).reshape(mp, group_rows, width)

        def in_grad(b, batch=None, half=None):
            span = COLS // group_rows
            rows = part_rows(batch)

            @pl.loop(*((0, width // COLS) if half is None else (half, half + 1)))
            def _(n):
                wk = [big[b, k, pl.ds(n * span, span)].reshape(COLS, width) for k in range(KERNEL)]
                g = [gtap(b, KERNEL - 1 - k, batch) for k in range(KERNEL)]
                acc[rows, cols_of(n)] = dot_nt(jnp.concatenate(g, axis=1), jnp.concatenate(wk, axis=1))

        def in_back(b, batch):
            x = x0 if b == 0 else x1

            @pl.loop(*part_windows(batch))
            def _(w):
                gn = acc[rows_of(w), :]
                hat, r = norm_parts(x[w].astype(F32))
                gbuf[0, 2 * b:2 * b + 1, :] += jnp.sum(gn * hat, axis=0, keepdims=True)
                value = mid[w] + norm_back(gn * gains[b, 0], hat, r)
                if b == 0:
                    x0[w] = from_phases(value).astype(BF)
                else:
                    ig1[w] = value.astype(BF)

                    def keep(r_, tile):
                        gout[w, pl.ds(r_ * q_count, q_count), :] = tile.astype(BF)
                    to_phases(value, keep)

        order = list(range(levels - 1, -1, -1))

        def region(ref, lead, kept, at):
            r0, rn, c0, cn = 0, half_rows, 0, width
            for j in range(levels - 1, kept - 1, -1):
                side = (at // (1 << j)) % 2
                if j >= 2:
                    cn //= 2
                    c0 = c0 + side * cn
                else:
                    rn //= 2
                    r0 = r0 + side * rn
            return r0, rn, c0, cn

        def grad_view(ref, group, half, part):
            j0, nj = group
            r0, rn, c0, cn = part
            rows = pl.ds(pl.multiple_of(half * half_rows + r0, TILE), rn)
            cols = slice(None) if cn == width else pl.ds(pl.multiple_of(c0, 128), cn)
            return ref.at[pl.ds(j0, nj), :, rows, cols]

        def add_into(group, half, part, other):
            j0, nj = group
            r0, rn, c0, cn = part
            rows = pl.ds(pl.multiple_of(half * half_rows + r0, TILE), rn)
            cols = slice(None) if cn == width else pl.ds(pl.multiple_of(c0, 128), cn)
            return j0, nj, rows, cols

        def accumulate(b, group, part, src):
            j0, nj, rows, cols = add_into(group, s, part, src)

            @pl.loop(j0, j0 + nj)
            def _(j):
                at = (slot(b), j, slice(None), rows, cols)
                big[at] = big[at] + src[j]

        def need_credit(n, which):
            if ggroups[n][0] == 0:
                pl.semaphore_wait(credit.at[n % per_grad, which], 1)

        def give_credit(n, which, device):
            if ggroups[n][0] == 1:
                pl.semaphore_signal(credit.at[n % per_grad, which], inc=1, device_id=device, device_id_type=MESH)

        def c_send(n):
            b, group = ggroups[n]
            need_credit(n, 0)
            src = grad_view(big.at[slot(b)], group, 1 - s, (0, half_rows, 0, width))
            begin(rcopy(src, recv_c.at[pl.ds(group[0], group[1])], rc_s.at[n], rc_r.at[n], sibling), None, n)

        def x_exchange(n, i):
            b, group = ggroups[n]
            j0, nj = group
            if i == 0:
                received(recv_c.at[pl.ds(j0, nj)], rc_r.at[n])
                accumulate(b, group, (0, half_rows, 0, width), recv_c)
                give_credit(n, 0, sibling)
            else:
                done = order[i - 1]
                received(recv_x[i - 1].at[pl.ds(j0, nj)], rx_r.at[n, i - 1])
                accumulate(b, group, region(None, None, done, place), recv_x[i - 1])
                give_credit(n, i, partner(done))
            if i < levels:
                j = order[i]
                need_credit(n, 1 + i)
                flip = place + (1 << j) - 2 * (1 << j) * bit(j)
                src = grad_view(big.at[slot(b)], group, s, region(None, None, j, flip))
                begin(rcopy(src, recv_x[i].at[pl.ds(j0, nj)], rx_s.at[n, i], rx_r.at[n, i], partner(j)), None, n)

        def z_send_pieces(n):
            j0, nj = ggroups[n][1]
            for k in range(1, mp):
                if n - per_grad not in z_first:
                    need_credit(n, levels + k)
                rcopy(big.at[shard_part(n, peer(k), region(None, None, 0, place))], recv_z.at[k - 1, pl.ds(j0, nj)],
                      rz_s.at[n], rz_r.at[n], dev(s, peer(k), d)).start()
            held = recv_z.at[:, pl.ds(j0, nj)]
            sends.append((rcopy(held, held, rz_s.at[n], rz_r.at[n], sibling), None, n))

        def z_take_pieces(n):
            b, (j0, nj) = ggroups[n]
            received(recv_z.at[:, pl.ds(j0, nj)], rz_r.at[n])
            total = big[shard_part(n, m, region(None, None, 0, place))].astype(F32)
            for k in range(1, mp):
                total = total + recv_z[k - 1, pl.ds(j0, nj)].astype(F32)
                if n + per_grad not in z_first:
                    give_credit(n, levels + k, dev(s, peer(mp - k), d))
            piece[b, pl.ds(j0, nj)] = total.astype(BF)
            spread(n)

        def keep_piece(n):
            b, (j0, nj) = ggroups[n]
            piece[b, pl.ds(j0, nj)] = big[shard_part(n, m, region(None, None, 0, place))]
            spread(n)

        def spread(n):
            b, group = ggroups[n]
            j0, nj = group
            r0, rn, c0, cn = region(None, None, 0, place)
            rows = pl.ds(pl.multiple_of(s * half_rows + r0, TILE), rn)
            cols = slice(None) if cn == width else pl.ds(pl.multiple_of(c0, 128), cn)
            dst = fin.at[pl.ds(j0, nj), rows, cols]
            src = piece.at[b, pl.ds(j0, nj)]

            pl.when(s == b)(pltpu.make_async_copy(src, dst, rf_r.at[0]).start)
            begin(rcopy(src, dst, rf_s.at[n, 0], rf_r.at[0], sibling), s != b, n)
            for o in range(1, dp):
                begin(rcopy(src, dst, rf_s.at[n, o], rf_r.at[0], dev(b, m, across(o))), None, n)

        def shard_part(n, mm, part):
            b, (j0, nj) = ggroups[n]
            r0, rn, c0, cn = part
            rows = pl.ds(pl.multiple_of(s * half_rows + r0, TILE), rn)
            cols = slice(None) if cn == width else pl.ds(pl.multiple_of(c0, 128), cn)
            if j0 < KERNEL:
                return (slot(b), pl.ds(j0, nj), mm, rows, cols)
            return (slot(b), j0 + mm, slice(None), rows, cols)

        side = (0, half_rows, 0, width)

        def z_pair(stage):
            if stage == 0:
                other = m + 1 - 2 * lax.rem(m, 2)
                return other, [(lax.rem(other, 2) + 2 * i, lax.rem(m, 2) + 2 * i, i) for i in range(2)]
            other = m + 2 - 4 * (m // 2)
            return other, [(other, m, 2)]

        def z_landing(n, i):
            return recv_zf.at[z_first[n], i, pl.ds(0, ggroups[n][1][1])]

        def z_first_send(n, stage):
            other, parts = z_pair(stage)
            at = z_order.index(n)
            for theirs, _, i in parts:
                begin(rcopy(big.at[shard_part(n, theirs, side)], z_landing(n, i),
                            zf_s.at[at, i], zf_r.at[at, i], dev(s, other, d)), None, n)

        def z_first_take(n, stage):
            other, parts = z_pair(stage)
            at = z_order.index(n)
            for _, mine, i in parts:
                received(z_landing(n, i), zf_r.at[at, i])
                where = shard_part(n, mine, side)
                big[where] = big[where] + recv_zf[z_first[n], i, pl.ds(0, ggroups[n][1][1])]

        def z_first_cross(n, i):
            j0, nj = ggroups[n][1]
            if i:
                done = order[i - 1]
                received(recv_x[i - 1].at[j0, pl.ds(0, nj)], rx_r.at[n, i - 1])
                where = shard_part(n, m, region(None, None, done, place))
                big[where] = big[where] + recv_x[i - 1][j0, pl.ds(0, nj)]
                give_credit(n, i, partner(done))
            if i < levels:
                j = order[i]
                need_credit(n, 1 + i)
                flip = place + (1 << j) - 2 * (1 << j) * bit(j)
                begin(rcopy(big.at[shard_part(n, m, region(None, None, j, flip))], recv_x[i].at[j0, pl.ds(0, nj)],
                            rx_s.at[n, i], rx_r.at[n, i], partner(j)), None, n)

        def z_first_chain(n):
            b, group = ggroups[n]
            j0, nj = group
            size = nj * width * width * 2 / 1e3
            c_send(n)
            yield post("core", size / 2, 500)
            received(recv_c.at[pl.ds(j0, nj)], rc_r.at[n])
            accumulate(b, group, side, recv_c)
            give_credit(n, 0, sibling)
            for stage in range(2):
                z_first_send(n, stage)
                yield post("z", size / 4 / (1 + stage), 50)
                z_first_take(n, stage)
            for i in range(levels):
                z_first_cross(n, i)
                yield post("xy", size / 16 / (1 << i), 100)
            z_first_cross(n, levels)
            keep_piece(n)
            post("xy", size / 2 / dp / mp * dp / 2, 100)

        def across(o):
            out = d
            for j in range(levels):
                if (o >> j) & 1:
                    out = out + (1 << j) - 2 * (1 << j) * ((d // (1 << j)) % 2)
            return out

        def reduce_chain(n):
            if n in z_first:
                yield from z_first_chain(n)
                return
            b, group = ggroups[n]
            size = group[1] * width * width * 2 / 1e3
            c_send(n)
            yield post("core", size / 2, 500)
            for i in range(levels):
                x_exchange(n, i)
                yield post("xy", size / 4 / (1 << i), 100)
            x_exchange(n, levels)
            z_send_pieces(n)
            yield post("z", 2 * size / 2 / dp, 100)
            z_take_pieces(n)
            post("xy", size / 2 / dp / mp * dp / 2, 100)

        first, second = range(per_block), range(per_block, 2 * per_block)
        for copy in loads:
            copy.wait()
        gbuf[0] = jnp.zeros((8, width), F32)
        received(gains.at[1 - s, 0], gn_r.at[0])
        received(gains.at[1 - s, 1], gn_r.at[1])
        work(2.5, first_norm, 0)
        stage_edges(xext)
        arrived = halo_send(0)
        for n in range(1, per_block):
            begin_gather(n)
        halo_wait(0, 0, arrived)
        work(0.5, fill_edges, xext)
        for g in range(3):
            complete([(0, g)])
            for n in range(width // COLS):
                work(1.0, conv_part, 0, range(3 * g, 3 * g + 3), None, n)
        for batch in range(batches):
            work(1.0, middle, 0, batch)
        complete([(0, 3)])
        for quarter in range(4):
            work(1.0, up, 0, None, quarter, 4)
        spill = [pltpu.make_async_copy(hid, sp_hid, loc.at[4]), pltpu.make_async_copy(slo, sp_slo, loc.at[5])]
        for copy in spill:
            copy.start()
        complete([(0, 4)])
        arrived = []
        for batch in range(batches):
            work(0.7, down, 0, batch)
            work(1.3, down_out, 0, batch)
            work(0.7, first_norm, 1, batch)
            arrived.append(halo_send(1, batch))
        send_home(x1, blk, 0, 0)
        zero_edges(xpad)
        zero_edges(gpad)
        work(2.5, branch_grad, 1)
        for batch in range(batches):
            halo_wait(1, batch, arrived[batch])
            if batch == 0:
                complete([(0, per_block + g) for g in range(3)])
            for n in range(width // COLS):
                work(1.0, conv_part, 1, range(KERNEL), batch, n)
            work(1.0, middle, 1, batch)
            if batch == 0:
                for copy in spill:
                    copy.wait()
                complete([(0, per_block + 3)])
            for half in range(2):
                work(0.7, up, 1, batch, half, 2)
        work(2.2, down_grad, 1)
        launch((1, 0), reduce_chain(0))
        work(1.5, transposed_ffn, 1)
        complete([(0, per_block + 4)])
        work(3.0, pre_grad, 1)
        work(2.2, up_grad, 1)
        launch((1, 1), reduce_chain(1))
        work(2.5, ffn_grad, 1)
        arrived = []
        for batch in range(batches):
            work(1.2, ffn_back, 1, batch)
            arrived.append(halo_send(3, batch))
        for g, group in enumerate(back_groups):
            work(0.7 * group[1], conv_grad, 1, group)
            launch((1, 2 + g), reduce_chain(2 + g))
        work(2.0, down, 1, None)
        work(1.0, down_out, 1, None)
        send_home(x2, blk, 1, 1)
        fetch = [pltpu.make_async_copy(sp_hid, hid, loc.at[6]), pltpu.make_async_copy(sp_slo, slo, loc.at[7])]
        for copy in fetch:
            copy.start()
        for batch in range(batches):
            halo_wait(3, batch, arrived[batch])
            work(1.8, in_grad, 1, batch)
            work(1.0, in_back, 1, batch)
        send_home(ig1, ing, 1, 3)
        flush(("gather", 1))
        work(2.5, branch_grad, 0)
        for copy in fetch:
            copy.wait()
        work(2.2, down_grad, 0)
        launch((1, per_grad), reduce_chain(per_grad))
        work(1.5, transposed_ffn, 0)
        work(3.0, pre_grad, 0)
        work(2.2, up_grad, 0)
        launch((1, per_grad + 1), reduce_chain(per_grad + 1))
        flush("halo")
        work(2.5, ffn_grad, 0)
        for batch in range(batches):
            work(1.2, ffn_back, 0, batch)
        stage_edges(gpad)
        arrived = halo_send(2)
        for g, group in enumerate(back_groups):
            work(0.7 * group[1], conv_grad, 0, group)
            launch((1, per_grad + 2 + g), reduce_chain(per_grad + 2 + g))
        halo_wait(2, 0, arrived)
        work(0.5, fill_edges, gpad)
        for half in range(width // COLS):
            work(2.5, in_grad, 0, None, half)
        for batch in range(batches):
            work(1.0, in_back, 0, batch)
        send_home(x0, ing, 0, 2)

        def gain_chain():
            own = 2 * d + s
            grecv[own] = gbuf[0]
            for o in range(dp):
                for ss in range(2):
                    if o or ss:
                        rcopy(gbuf.at[0], grecv.at[own], gn_s.at[2], gn_r.at[2],
                              dev(s + ss - 2 * s * ss, m, across(o))).start()
            held = grecv.at[pl.ds(0, 2 * dp - 1)]
            sends.append((rcopy(held, held, gn_s.at[2], gn_r.at[2], sibling), None, "gains"))
            yield clock["now"] + 2 * LATENCY
            received(held, gn_r.at[2])
            total = grecv[0]
            for i in range(1, 2 * dp):
                total = total + grecv[i]
            gbuf[1] = total
            for k in range(1, mp):
                rcopy(gbuf.at[1], gz.at[k - 1], gn_s.at[3], gn_r.at[3], dev(s, peer(k), d)).start()
            sends.append((rcopy(gz, gz, gn_s.at[3], gn_r.at[3], sibling), None, "gains"))
            yield clock["now"] + 2 * LATENCY
            received(gz, gn_r.at[3])
            for k in range(1, mp):
                total = total + gz[k - 1]
            gbuf[2] = total

        launch((2, 0), gain_chain())
        for n in range(nwg):
            z_flush(n)
        flush(("gather", 0))
        flush("halo")
        for n in range(ngg):
            if (1, n) not in chains:
                flush(n)
        complete(list(chains))
        out = pltpu.make_async_copy(
            gbuf.at[2, :, pl.ds(pl.multiple_of(m * group_rows, group_rows), group_rows)], gout_sum, loc.at[0])
        out.start()
        received(fin, rf_r.at[0])
        flush()
        sent_home(x1, blk, 0, 0)
        sent_home(x2, blk, 1, 1)
        sent_home(x0, ing, 0, 2)
        sent_home(ig1, ing, 1, 3)
        out.wait()

    vm = pltpu.VMEM
    dma = pltpu.SemaphoreType.DMA
    plain = (nw, seq, width)
    flat = (rows_all, width)

    def recv_shape(i):
        r, c = half_rows, width
        for j in range(levels - 1, levels - 2 - i, -1):
            if j >= 2:
                c //= 2
            else:
                r //= 2
        return (nblk, mp, r, c)

    piece_shape = (nblk, recv_shape(levels - 1)[2], recv_shape(levels - 1)[3])
    scratch = [
        vm((3, nblk, mp, group_rows, width), BF),
        vm((nblk, mp, half_rows, width), BF),
        vm((mp - 1,) + piece_shape, BF),
        vm((max(1, min(2, len(Z_FIRST))), 3, mp, half_rows, width), BF),
        vm((2,) + piece_shape, BF),
        vm((nw, 2 * seq, width), BF),
        vm((nw, 2 * margin + seq, width), BF),
        vm((nw, 2 * margin + seq, width), BF),
        vm((rows_all, mp * width), BF),
        vm((rows_all, mp * width), BF),
        vm(plain, BF),
        vm(plain, BF),
        vm(plain, BF),
        vm((2,) + plain, BF),
        vm((2,) + flat, BF),
        vm((2,) + plain, BF),
        vm(plain, BF),
        vm(flat, BF),
        vm((width, rows_all), BF),
        vm((width, rows_all), BF),
        vm(flat, F32),
        vm(plain, F32),
        vm(plain, BF),
        vm((2, 2, 1, width), F32),
        vm((width // 128, seq, 128), F32),
        vm((2 * HALF, q_count + 16, width), F32),
        vm((2, nw, 8, width), F32),
        vm((2, nw, 8, width), F32),
        vm((3, 8, width), F32),
        vm((2 * dp, 8, width), F32),
        vm((mp - 1, 8, width), F32),
    ] + [vm(recv_shape(i), BF) for i in range(levels)] + [
        dma((per_block, mp - 1, 2)), dma((nwg, mp - 1)), dma((nwg,)),
        dma((nwg, levels)), dma((nwg, levels)),
        dma((nwg,)), dma((nwg,)),
        dma((per_block,)), dma((per_block,)), dma((per_block,)),
        dma((ngg,)), dma((ngg,)),
        dma((ngg, levels)), dma((ngg, levels)),
        dma((ngg,)), dma((ngg,)),
        dma((1 + len(z_first), 3)), dma((1 + len(z_first), 3)),
        dma((ngg, dp)), dma((1,)),
        dma((4,)), dma((4,)),
        dma((4, batches, 2)), dma((4, batches, 2)),
        dma((4,)), dma((4,)),
        dma((8,)),
        pltpu.SemaphoreType.REGULAR((per_grad, levels + mp)),
    ]
    return body, scratch


def per_device(tokens, valid, conv_weight, gain_one, gain_two, up_weight, down_weight, cotangent):
    mp = lax.axis_size("mp")
    dp = lax.axis_size("dp")
    windows, seq, width = tokens.shape
    nw = windows // 2
    rows = width // mp
    body, scratch = make_kernel(mp, dp, nw, seq, width)
    conv = conv_weight[0].reshape(KERNEL, mp, rows, rows)
    up = up_weight[0].reshape(mp, rows, width)
    down = down_weight[0].reshape(mp, rows, width)
    nblk = KERNEL + 2 * mp
    anywhere = pl.BlockSpec(memory_space=pl.ANY)
    blk, ing, fin, sums, _, _ = pl.pallas_call(
        body,
        out_shape=(
            jax.ShapeDtypeStruct(tokens.shape, BF),
            jax.ShapeDtypeStruct(tokens.shape, BF),
            jax.ShapeDtypeStruct((nblk, rows, width), BF),
            jax.ShapeDtypeStruct((8, rows), F32),
            jax.ShapeDtypeStruct((nw * seq, mp * width), BF),
            jax.ShapeDtypeStruct((nw * seq, mp * width), BF),
        ),
        in_specs=[anywhere] * 2 + [pl.BlockSpec(memory_space=pltpu.SMEM)] + [anywhere] * 5,
        out_specs=[anywhere] * 6,
        scratch_shapes=scratch,
        compiler_params=pltpu.CompilerParams(
            collective_id=0, has_side_effects=True, vmem_limit_bytes=64 * 1024 * 1024 - 64 * 1024
        ),
    )(tokens, cotangent, valid, gain_one, gain_two, conv, up, down)
    return finalize(mp, blk, ing, fin, sums)


def finalize(mp, blk, ing, fin, sums):
    nblk, rows, width = fin.shape

    def body(blk_in, ing_in, fin_in, sums_in, blk_out, ing_out, conv_out, one_out, two_out, up_out, down_out,
             held, conv, up, down, acts, sem):
        moves = [pltpu.make_async_copy(blk_in, acts.at[0], sem.at[0]),
                 pltpu.make_async_copy(ing_in, acts.at[1], sem.at[1])]
        parts = [(0, KERNEL), (KERNEL, mp), (KERNEL + mp, mp)]
        reads = [pltpu.make_async_copy(fin_in.at[pl.ds(a, n)], held.at[pl.ds(a, n)], sem.at[2 + i])
                 for i, (a, n) in enumerate(parts)]
        for copy in reads[:1] + moves + reads[1:]:
            copy.start()
        first = lax.axis_index("section") == 0
        one_out[...] = jnp.where(first, sums_in[0:1, :], sums_in[2:3, :])
        two_out[...] = jnp.where(first, sums_in[1:2, :], sums_in[3:4, :])
        writes = []

        def store(src, dst, at):
            copy = pltpu.make_async_copy(src, dst, sem.at[at])
            copy.start()
            writes.append(copy)

        reads[0].wait()
        for k in range(KERNEL):
            conv[k] = held[k].T.astype(F32)
            if k % 3 == 2:
                store(conv.at[pl.ds(k - 2, 3)], conv_out.at[0, pl.ds(k - 2, 3)], 5 + k // 3)
            if k < 2:
                moves[k].wait()
                store(acts.at[k], (blk_out, ing_out)[k].at[0], 10 + k)
        reads[2].wait()
        for j in range(mp):
            down[:, j * rows:(j + 1) * rows] = held[KERNEL + mp + j].T.astype(F32)
        store(down, down_out.at[0], 8)
        reads[1].wait()
        for j in range(mp):
            up[j * rows:(j + 1) * rows, :] = held[KERNEL + j].astype(F32)
        store(up, up_out.at[0], 9)
        for copy in writes:
            copy.wait()

    anywhere = pl.BlockSpec(memory_space=pl.ANY)
    vmem = pl.BlockSpec(memory_space=pltpu.VMEM)
    square = (mp * rows, width)
    return pl.pallas_call(
        body,
        out_shape=(
            jax.ShapeDtypeStruct((1,) + blk.shape, BF),
            jax.ShapeDtypeStruct((1,) + ing.shape, BF),
            jax.ShapeDtypeStruct((1, KERNEL, width, rows), F32),
            jax.ShapeDtypeStruct((1, rows), F32),
            jax.ShapeDtypeStruct((1, rows), F32),
            jax.ShapeDtypeStruct((1,) + square, F32),
            jax.ShapeDtypeStruct((1, width, mp * rows), F32),
        ),
        in_specs=[anywhere, anywhere, anywhere, vmem],
        out_specs=[anywhere, anywhere, anywhere, vmem, vmem, anywhere, anywhere],
        scratch_shapes=[
            pltpu.VMEM(fin.shape, BF),
            pltpu.VMEM((KERNEL, width, rows), F32),
            pltpu.VMEM(square, F32),
            pltpu.VMEM((width, mp * rows), F32),
            pltpu.VMEM((2,) + blk.shape, BF),
            pltpu.SemaphoreType.DMA((12,)),
        ],
        compiler_params=pltpu.CompilerParams(vmem_limit_bytes=64 * 1024 * 1024 - 64 * 1024),
    )(blk, ing, fin, sums)


def solution(mesh):
    in_specs = (
        P("dp", "mp", None),
        P("dp"),
        P("section", None, None, "mp"),
        P("section", None),
        P("section", None),
        P("section", None, "mp"),
        P("section", "mp", None),
        P("dp", "mp", None),
    )
    out_specs = (
        P("section", "dp", "mp", None),
        P("section", "dp", "mp", None),
        P("section", None, None, "mp"),
        P("section", "mp"),
        P("section", "mp"),
        P("section", None, "mp"),
        P("section", "mp", None),
    )
    return jax.shard_map(
        per_device, mesh=mesh, in_specs=in_specs, out_specs=out_specs, check_vma=False
    )
```
